32 devices in a mesh: groups: 2 (over y), expert: 8 (over z, x), tensor: 2 (over core).
Axes of the slice: x: 2, y: 2, z: 4, core: 2. Of those that a mesh axis runs over, the one named last changes fastest.
Arguments:
- tokens: bfloat16 [2, 256, 3584], P(None, ('groups', 'expert')), parts along dimension 1, may hold values from -6 to 6
- routes: int32 [2, 256, 8], P(None, ('groups', 'expert')), parts along dimension 1, may hold values from 0 to 63, as said below
- gating: float32 [2, 256, 8], P(None, ('groups', 'expert')), parts along dimension 1, may hold values from 0.05 to 0.5
- gate_weight: bfloat16 [64, 3584, 1024], P('expert', None, 'tensor'), may hold values from -0.09375 to 0.09375
- up_weight: bfloat16 [64, 3584, 1024], P('expert', None, 'tensor'), may hold values from -0.09375 to 0.09375
- down_weight: bfloat16 [64, 1024, 3584], P('expert', 'tensor'), may hold values from -0.1875 to 0.1875
Outputs:
- combined: bfloat16 [2, 256, 3584], P(None, ('groups', 'expert'), 'tensor'), parts along dimension 1
The draws below stay inside these ranges and needn't reach their ends.
There are 2 independent parts, one for each index of `groups`. The reference program is written for one: setup_inputs(seed, part) draws one part's arguments, and reference() takes and returns one part's arrays. A program takes and returns all parts, laid end to end along the dimension named above; an argument that names none is the same for every part. Nothing has to cross between parts.
Inputs may be any that keep to these rules, and one draw needn't show every extreme that they name: `routes`: each row names 8 different experts. In every step the same 1 expert is named by exactly 10 of the rows of every device (aligned blocks of 16 rows). Every other expert is named by at most 2 rows of one device, and in every block some expert reaches 2.
All inputs are finite; a program needn't handle non-finite values.
Results may differ from the reference program's by a relative error of at most 0.0058.
Values may be sent and summed in bfloat16 or wider, within the bound.
No kernel may reach another device: no remote copies, remote signals or barrier semaphores. Data moves between devices by JAX's collectives and lax.ppermute only.
A program may use at most 256 MiB of HBM per device.

```python
import math
import jax
import jax.numpy as jnp
from jax import lax

D = 3584
FF = 1024
TOPK = 8
HOT = 1
STEPS = 2
TOK_DEV = 16
TOKENS = 128
EXPERTS = 64
CAP_HOT = 10
CAP = 2
N_TENSOR = 2


def draw_routes(key, part):
    key = jax.random.fold_in(key, 11)
    shuffled = jax.random.permutation(jax.random.fold_in(key, 1), EXPERTS).astype(jnp.int32)
    hot_ids = shuffled[:HOT]
    cold_ids = shuffled[HOT:]
    slot_total = TOPK * TOK_DEV
    item_index = jnp.arange(slot_total, dtype=jnp.int32)
    hot_items = hot_ids[jnp.minimum(item_index // CAP_HOT, HOT - 1)]
    cold_position = jnp.maximum(item_index - HOT * CAP_HOT, 0) // CAP

    def one_block(block_key):
        first_key, second_key, third_key = jax.random.split(block_key, 3)
        cold_order = jax.random.permutation(first_key, cold_ids)
        cold_items = cold_order[jnp.minimum(cold_position, EXPERTS - HOT - 1)]
        items = jnp.where(item_index < HOT * CAP_HOT, hot_items, cold_items)
        table_rows = items.reshape(TOPK, TOK_DEV).T
        row_order = jax.random.permutation(second_key, TOK_DEV)
        table_rows = table_rows[row_order]
        scores = jax.random.randint(third_key, (TOK_DEV, TOPK), 0, 1 << 20) * TOPK + jnp.arange(TOPK, dtype=jnp.int32)[None, :]
        column_order = jnp.argsort(scores, axis=1, stable=True)
        return jnp.take_along_axis(table_rows, column_order, axis=1)
    block_keys = jax.random.split(jax.random.fold_in(key, 2), STEPS * (TOKENS // TOK_DEV))
    blocks = jax.vmap(one_block)(block_keys)
    return blocks.reshape(STEPS, TOKENS, TOPK).astype(jnp.int32)


def levels(stream_key, dims, shards, least, largest):
    factor_of, own = 1.0, jax.random.fold_in(stream_key, 6)
    for dim, blocks in shards:
        draws = jnp.exp(jax.random.uniform(jax.random.fold_in(own, dim), (blocks,), jnp.float32, least / len(shards), largest / len(shards)))
        factor_of = factor_of * jnp.repeat(draws, dims[dim] // blocks).reshape([-1 if axis == dim else 1 for axis in range(len(dims))])
    return factor_of


def bell_draw(key, dims, deviation, most, cuts=(), kind=jnp.bfloat16):
    factor_of = levels(key, dims, cuts, -0.22, 0.18) if cuts else 1.0
    array = jax.random.normal(key, dims, jnp.float32) * deviation * factor_of
    return jnp.minimum(jnp.maximum(array, -most), most).astype(kind)


def setup_inputs(seed: int = 0, part: int = 0) -> dict:
    streams_of = jax.random.split(jax.random.key(seed), 7)
    own_keys = jax.random.split(jax.random.fold_in(streams_of[6], part), 7)
    tokens = bell_draw(own_keys[0], (STEPS, TOKENS, D), 1.0, 6.0, ((1, 8),))
    routes = draw_routes(jax.random.fold_in(jax.random.fold_in(streams_of[6], part), 71), part)
    gating = jnp.clip(jnp.exp(math.log(0.5) - 2.3025851 * jax.random.uniform(own_keys[2], (STEPS, TOKENS, TOPK), jnp.float32) ** levels(own_keys[2], (STEPS, TOKENS, TOPK), ((1, 8),), -0.2, 0.2)), 0.05, 0.5)
    gate_weight = bell_draw(streams_of[3], (EXPERTS, D, FF), D ** -0.5, 0.09375, ((0, 8), (2, 2)))
    up_weight = bell_draw(streams_of[4], (EXPERTS, D, FF), D ** -0.5, 0.09375, ((0, 8), (2, 2)))
    down_weight = bell_draw(streams_of[5], (EXPERTS, FF, D), FF ** -0.5, 0.1875, ((0, 8), (1, 2)))
    return {"tokens": tokens, "routes": routes, "gating": gating, "gate_weight": gate_weight, "up_weight": up_weight, "down_weight": down_weight}


def expert_forward(row_data, w_gate, w_up, w_down):
    gate_proj = jnp.dot(row_data, w_gate, preferred_element_type=jnp.float32)
    up_proj = jnp.dot(row_data, w_up, preferred_element_type=jnp.float32)
    active = (jax.nn.silu(gate_proj) * up_proj).astype(jnp.bfloat16)
    core_width = w_down.shape[0] // N_TENSOR
    summed = jnp.zeros((row_data.shape[0], w_down.shape[1]), jnp.float32)
    for core_index in range(N_TENSOR):
        lower = core_index * core_width
        partial_value = jnp.dot(active[:, lower:lower + core_width], w_down[lower:lower + core_width], preferred_element_type=jnp.float32)
        summed = summed + partial_value.astype(jnp.bfloat16).astype(jnp.float32)
    return summed


def one_step(token_rows, route_rows, gate_rows, gate_weight, up_weight, down_weight):
    row_block = 64
    flat_ids = route_rows.reshape(-1).astype(jnp.int32)
    pair_count = flat_ids.shape[0]
    experts = gate_weight.shape[0]
    expert_ids = jnp.arange(experts, dtype=jnp.int32)
    sorted_pairs = jnp.argsort(flat_ids, stable=True).astype(jnp.int32)
    counts = jnp.sum((flat_ids[:, None] == expert_ids[None, :]).astype(jnp.int32), axis=0).astype(jnp.int32)
    starts = (jnp.cumsum(counts) - counts).astype(jnp.int32)
    nblocks = ((counts + row_block - 1) // row_block).astype(jnp.int32)
    block_ends = jnp.cumsum(nblocks).astype(jnp.int32)
    total_blocks = pair_count // row_block + experts
    padded_pairs = jnp.concatenate([sorted_pairs, jnp.zeros((row_block,), jnp.int32)])
    flat_gates = gate_rows.reshape(-1)
    lanes = jnp.arange(row_block, dtype=jnp.int32)

    def visit(running, block_index):
        owner_index = jnp.sum((block_ends <= block_index).astype(jnp.int32)).astype(jnp.int32)
        expert = jnp.minimum(owner_index, experts - 1).astype(jnp.int32)
        first_block = block_ends[expert] - nblocks[expert]
        offset = ((block_index - first_block) * row_block).astype(jnp.int32)
        picked = lax.dynamic_slice_in_dim(padded_pairs, (starts[expert] + offset).astype(jnp.int32), row_block)
        live_rows = (lanes + offset < counts[expert]) & (owner_index < experts)
        token_index = (picked // TOPK).astype(jnp.int32)
        expert_out = expert_forward(token_rows[token_index], gate_weight[expert], up_weight[expert], down_weight[expert])
        weight = jnp.where(live_rows, flat_gates[picked], jnp.zeros_like(flat_gates[picked]))
        running = running.at[token_index].add(expert_out * weight[:, None])
        return running, None

    start_sum = jnp.zeros((token_rows.shape[0], token_rows.shape[1]), jnp.float32)
    running, _ = lax.scan(visit, start_sum, jnp.arange(total_blocks, dtype=jnp.int32))
    return running.astype(jnp.bfloat16)


def reference(tokens, routes, gating, gate_weight, up_weight, down_weight):
    results = []
    for step_index in range(STEPS):
        results.append(one_step(tokens[step_index], routes[step_index], gating[step_index], gate_weight, up_weight, down_weight))
    return jnp.stack(results)
```

```python
import functools

import jax
import jax.numpy as jnp
from jax import lax
from jax.experimental import pallas as pl
from jax.experimental.pallas import tpu as pltpu
from jax.sharding import PartitionSpec as P

META = 128


def expert_kernel(
    topk,
    cap_cold,
    cap_hot,
    place_ref,
    mine_ref,
    theirs_ref,
    gate_ref,
    up_ref,
    down_ref,
    keep_ref,
    send_ref,
    rank_rows,
    weight_rows,
    counts,
    gathered,
    returned,
    hot_rows,
    hot_sum,
    hot_seen,
):
    step = pl.program_id(0)
    experts_here = pl.num_programs(0)
    rows = mine_ref.shape[0]
    half = mine_ref.shape[1] - META
    core = place_ref[1]
    my_half = pl.ds(pl.multiple_of(core * half, 128), half)
    other_half = pl.ds(pl.multiple_of((1 - core) * half, 128), half)

    def gather(selector, target):
        target[:, my_half] = jnp.dot(
            selector, mine_ref[:, :half], preferred_element_type=jnp.float32
        ).astype(jnp.bfloat16)
        target[:, other_half] = jnp.dot(
            selector, theirs_ref[:, :half], preferred_element_type=jnp.float32
        ).astype(jnp.bfloat16)

    def pick(expert, count):
        slots = lax.broadcasted_iota(jnp.int32, (count, rows), 0).astype(jnp.float32)
        return jnp.where(rank_rows[pl.ds(expert, 1), :] == slots, 1.0, 0.0)

    @pl.when(step == 0)
    def _():
        hot_seen[0] = 0
        meta = mine_ref[:, half:].astype(jnp.float32)
        lane = lax.broadcasted_iota(jnp.int32, (rows, 128), 1)
        wanted = (place_ref[0] * experts_here + lane).astype(jnp.float32)
        member = jnp.zeros((rows, 128), jnp.float32)
        weight = jnp.zeros((rows, 128), jnp.float32)
        for k in range(topk):
            gate = (
                meta[:, topk + k : topk + k + 1]
                + meta[:, 2 * topk + k : 2 * topk + k + 1]
                + meta[:, 3 * topk + k : 3 * topk + k + 1]
            )
            hit = (meta[:, k : k + 1] == wanted) & (lane < experts_here)
            member = member + jnp.where(hit, 1.0, 0.0)
            weight = weight + jnp.where(hit, gate, 0.0)
        earlier = (
            lax.broadcasted_iota(jnp.int32, (rows, rows), 1)
            < lax.broadcasted_iota(jnp.int32, (rows, rows), 0)
        )
        rank = jnp.dot(
            jnp.where(earlier, 1.0, 0.0).astype(jnp.bfloat16),
            member.astype(jnp.bfloat16),
            preferred_element_type=jnp.float32,
        )
        rank_rows[...] = jnp.where(member > 0.0, rank, -1.0).T
        weight_rows[...] = weight.T
        totals = jnp.sum(member, axis=0, keepdims=True)
        for e in range(counts.shape[0]):
            counts[e] = totals[0, e].astype(jnp.int32)
        selector = jnp.concatenate(
            [pick(e, cap_cold) for e in range(counts.shape[0])], axis=0
        ).astype(jnp.bfloat16)
        gather(selector, gathered)

    def forward(row_data, weight_column):
        gate_proj = jnp.dot(row_data, gate_ref[0], preferred_element_type=jnp.float32)
        up_proj = jnp.dot(row_data, up_ref[0], preferred_element_type=jnp.float32)
        active = (jax.nn.silu(gate_proj) * up_proj).astype(jnp.bfloat16)
        partial = jnp.dot(active, down_ref[0], preferred_element_type=jnp.float32)
        return (partial * weight_column).astype(jnp.bfloat16)

    block = pl.ds(pl.multiple_of(step * cap_cold, cap_cold), cap_cold)
    is_hot = counts[step] > cap_cold

    @pl.when(jnp.logical_not(is_hot))
    def _():
        weight_column = jnp.sum(
            pick(step, cap_cold) * weight_rows[pl.ds(step, 1), :], axis=1, keepdims=True
        )
        returned[block, :] = forward(gathered[block, :], weight_column)

    @pl.when(is_hot)
    def _():
        selector = pick(step, cap_hot)
        gather(selector.astype(jnp.bfloat16), hot_rows)
        weight_column = jnp.sum(
            selector * weight_rows[pl.ds(step, 1), :], axis=1, keepdims=True
        )
        returned[block, :] = jnp.zeros((cap_cold, returned.shape[1]), jnp.bfloat16)
        hot_rows[...] = forward(hot_rows[...], weight_column)
        spread = jnp.dot(
            selector.T.astype(jnp.bfloat16), hot_rows[...], preferred_element_type=jnp.float32
        )

        @pl.when(hot_seen[0] == 0)
        def _():
            hot_sum[...] = spread

        @pl.when(hot_seen[0] != 0)
        def _():
            hot_sum[...] += spread

        hot_seen[0] = 1

    @pl.when(step == experts_here - 1)
    def _():
        selector = jnp.concatenate(
            [pick(e, cap_cold) for e in range(counts.shape[0])], axis=0
        )
        spread = selector.T.astype(jnp.bfloat16)
        for columns, out_ref in ((my_half, keep_ref), (other_half, send_ref)):
            value = jnp.dot(
                spread, returned[:, columns], preferred_element_type=jnp.float32
            )
            out_ref[...] = value.astype(jnp.bfloat16)

            @pl.when(hot_seen[0] != 0)
            def _():
                out_ref[...] = (value + hot_sum[:, columns]).astype(jnp.bfloat16)


def run_experts(place, mine, theirs, gate_weight, up_weight, down_weight, topk, cap_cold, cap_hot):
    rows = mine.shape[0]
    half = mine.shape[1] - META
    experts_here, features, hidden = gate_weight.shape
    out = jax.ShapeDtypeStruct((rows, half), jnp.bfloat16)
    whole = lambda shape: pl.BlockSpec(shape, lambda e, *_: (0,) * len(shape))
    return pl.pallas_call(
        functools.partial(expert_kernel, topk, cap_cold, cap_hot),
        grid_spec=pltpu.PrefetchScalarGridSpec(
            num_scalar_prefetch=1,
            grid=(experts_here,),
            in_specs=[
                whole(mine.shape),
                whole(theirs.shape),
                pl.BlockSpec((1, features, hidden), lambda e, *_: (e, 0, 0)),
                pl.BlockSpec((1, features, hidden), lambda e, *_: (e, 0, 0)),
                pl.BlockSpec((1, hidden, features), lambda e, *_: (e, 0, 0)),
            ],
            out_specs=[whole((rows, half)), whole((rows, half))],
            scratch_shapes=[
                pltpu.VMEM((128, rows), jnp.float32),
                pltpu.VMEM((128, rows), jnp.float32),
                pltpu.SMEM((experts_here,), jnp.int32),
                pltpu.VMEM((experts_here * cap_cold, features), jnp.bfloat16),
                pltpu.VMEM((experts_here * cap_cold, features), jnp.bfloat16),
                pltpu.VMEM((cap_hot, features), jnp.bfloat16),
                pltpu.VMEM((rows, features), jnp.float32),
                pltpu.SMEM((1,), jnp.int32),
            ],
        ),
        out_shape=[out, out],
        compiler_params=pltpu.CompilerParams(vmem_limit_bytes=56 * 1024 * 1024),
        cost_estimate=pl.CostEstimate(
            flops=6 * rows * features * hidden,
            bytes_accessed=6 * experts_here * features * hidden,
            transcendentals=0,
        ),
    )(place, mine, theirs, gate_weight, up_weight, down_weight)


def local(tokens, routes, gating, gate_weight, up_weight, down_weight):
    step_count, tok_dev, features = tokens.shape
    topk = routes.shape[2]
    devices = lax.axis_size("expert")
    pairs = devices // 2
    half = features // 2
    rows_here = step_count * tok_dev
    core = lax.axis_index("tensor")
    swap = [(0, 1), (1, 0)]
    flip = [(i, i ^ 1) for i in range(devices)]

    def shift(value, k):
        return lax.ppermute(
            value, "expert", [(i, (i + 2 * k) % devices) for i in range(devices)]
        )

    top = gating.astype(jnp.bfloat16)
    rest = gating - top.astype(jnp.float32)
    middle = rest.astype(jnp.bfloat16)
    low = (rest - middle.astype(jnp.float32)).astype(jnp.bfloat16)
    meta = jnp.concatenate([routes.astype(jnp.bfloat16), top, middle, low], axis=2)
    meta = jnp.pad(meta, ((0, 0), (0, 0), (0, META - meta.shape[2])))
    mine = jnp.concatenate(
        [lax.dynamic_slice_in_dim(tokens, core * half, half, 2), meta], axis=2
    ).reshape(rows_here, half + META)

    mine = jnp.concatenate([mine] + [shift(mine, k) for k in range(1, pairs)])
    mine = jnp.concatenate([mine, lax.ppermute(mine, "expert", flip)])
    theirs = lax.ppermute(mine, "tensor", swap)

    place = jnp.stack([lax.axis_index("expert"), core]).astype(jnp.int32)
    keep, send = run_experts(
        place,
        mine,
        theirs,
        gate_weight,
        up_weight,
        down_weight,
        topk,
        step_count * devices * 2,
        step_count * devices * (tok_dev * 5 // 8),
    )

    f32 = jnp.float32
    both = keep.astype(f32) + lax.ppermute(send, "tensor", swap).astype(f32)
    both = both.reshape(2, pairs, rows_here, half)
    column = both[0] + lax.ppermute(both[1].astype(jnp.bfloat16), "expert", flip).astype(f32)
    total = column[0]
    for k in range(1, pairs):
        total = total + shift(column[k].astype(jnp.bfloat16), pairs - k).astype(f32)
    return total.astype(jnp.bfloat16).reshape(step_count, tok_dev, half)


def expert_block(received, w_gate, w_up, w_down):
    gate_proj = jnp.einsum("nemd,edf->nemf", received, w_gate, preferred_element_type=jnp.float32)
    up_proj = jnp.einsum("nemd,edf->nemf", received, w_up, preferred_element_type=jnp.float32)
    active = (jax.nn.silu(gate_proj) * up_proj).astype(jnp.bfloat16)
    return jnp.einsum("nemf,efd->nemd", active, w_down, preferred_element_type=jnp.float32).astype(
        jnp.bfloat16
    )


def pair_ranks(flat_ids):
    pair_count = flat_ids.shape[0]
    positions = jnp.arange(pair_count, dtype=jnp.int32)
    earlier = (flat_ids[:, None] == flat_ids[None, :]) & (positions[None, :] < positions[:, None])
    return jnp.sum(earlier.astype(jnp.int32), axis=1)


def pack_rows(slot_of_pair, slot_count, topk, row_data):
    slot_ids = jnp.arange(slot_count, dtype=jnp.int32)
    hits = (slot_ids[:, None] == slot_of_pair[None, :]).reshape(slot_count, -1, topk)
    selector = jnp.any(hits, axis=2).astype(jnp.bfloat16)
    return jnp.dot(selector, row_data, preferred_element_type=jnp.float32).astype(jnp.bfloat16)


def local_by_slots(tokens, routes, gating, gate_weight, up_weight, down_weight):
    step_count, tok_dev, feature_count = tokens.shape
    topk = routes.shape[2]
    experts_here = gate_weight.shape[0]
    device_count = lax.axis_size("expert")
    experts = experts_here * device_count
    hot_cap = tok_dev * 5 // 8
    outputs = []
    for step_index in range(step_count):
        token_rows = tokens[step_index]
        flat_ids = routes[step_index].reshape(-1)
        ranks = pair_ranks(flat_ids)
        send_slot = flat_ids * hot_cap + ranks
        send_buffer = pack_rows(send_slot, experts * hot_cap, topk, token_rows).reshape(
            device_count, experts_here, hot_cap, token_rows.shape[1]
        )
        results = expert_block(
            lax.all_to_all(send_buffer, "expert", split_axis=0, concat_axis=0, tiled=True),
            gate_weight,
            up_weight,
            down_weight,
        )
        returned = lax.all_to_all(
            results, "expert", split_axis=0, concat_axis=0, tiled=True
        ).reshape(experts * hot_cap, feature_count)
        pair_rows = returned[send_slot]
        weighted = (
            pair_rows.astype(jnp.float32).reshape(tok_dev, topk, feature_count)
            * gating[step_index][:, :, None]
        )
        running = jnp.sum(weighted, axis=1)
        outputs.append(
            lax.psum_scatter(running, "tensor", scatter_dimension=1, tiled=True).astype(
                jnp.bfloat16
            )
        )
    return jnp.stack(outputs)


def solution(mesh):
    body = local if mesh.shape["expert"] <= 16 else local_by_slots
    in_specs = (
        P(None, ("groups", "expert"), None),
        P(None, ("groups", "expert"), None),
        P(None, ("groups", "expert"), None),
        P("expert", None, "tensor"),
        P("expert", None, "tensor"),
        P("expert", "tensor", None),
    )
    out_specs = P(None, ("groups", "expert"), "tensor")
    return jax.shard_map(body, mesh=mesh, in_specs=in_specs, out_specs=out_specs, check_vma=False)
```

```python
import functools

import jax
import jax.numpy as jnp
from jax import lax
from jax.experimental import pallas as pl
from jax.experimental.pallas import tpu as pltpu
from jax.sharding import PartitionSpec as P

META = 128
AHEAD = 2
RING = 4
MIB = 1024 * 1024


def in_vmem(value):
    return pltpu.with_memory_space_constraint(value, pltpu.VMEM)


def in_hbm(value):
    return pltpu.with_memory_space_constraint(value, pltpu.HBM)


VMEM_SPEC = pl.BlockSpec(memory_space=pltpu.VMEM)
HBM_SPEC = pl.BlockSpec(memory_space=pl.ANY)
DONE = pltpu.VMEM((8, 128), jnp.float32)
SMALL = pl.CostEstimate(flops=1, bytes_accessed=1, transcendentals=0)


def run_copies(copies):
    for copy in copies:
        copy.start()
    for copy in copies:
        copy.wait()


def prepare(core, tokens, routes, gating):
    step_count, tok_dev, features = tokens.shape
    topk = routes.shape[2]
    half = features // 2

    def kernel(core_ref, tokens_ref, routes_hbm, gating_hbm, out_ref, routes_ref, gating_ref, sems):
        columns = pl.ds(pl.multiple_of(core_ref[0] * half, 128), half)
        copies = [
            pltpu.make_async_copy(
                tokens_ref.at[s, :, columns],
                out_ref.at[s * tok_dev : (s + 1) * tok_dev, :half],
                sems.at[s],
            )
            for s in range(step_count)
        ]
        small = [
            pltpu.make_async_copy(routes_hbm, routes_ref, sems.at[step_count]),
            pltpu.make_async_copy(gating_hbm, gating_ref, sems.at[step_count + 1]),
        ]
        for copy in small + copies:
            copy.start()
        for copy in small:
            copy.wait()
        for s in range(step_count):
            weight = gating_ref[s].T
            top = weight.astype(jnp.bfloat16)
            rest = weight - top.astype(jnp.float32)
            middle = rest.astype(jnp.bfloat16)
            low = rest - middle.astype(jnp.float32)
            parts = [
                routes_ref[s].astype(jnp.float32).T,
                top.astype(jnp.float32),
                middle.astype(jnp.float32),
                low,
                jnp.zeros((tok_dev, META - 4 * topk), jnp.float32),
            ]
            out_ref[s * tok_dev : (s + 1) * tok_dev, half:] = jnp.concatenate(
                parts, axis=1
            ).astype(jnp.bfloat16)
        for copy in copies:
            copy.wait()

    return pl.pallas_call(
        kernel,
        in_specs=[pl.BlockSpec(memory_space=pltpu.SMEM), HBM_SPEC, HBM_SPEC, HBM_SPEC],
        out_specs=VMEM_SPEC,
        out_shape=pltpu.VMEM((step_count * tok_dev, half + META), jnp.bfloat16),
        scratch_shapes=[
            pltpu.VMEM((step_count, topk, tok_dev), jnp.int32),
            pltpu.VMEM((step_count, topk, tok_dev), jnp.float32),
            pltpu.SemaphoreType.DMA((step_count + 2,)),
        ],
        compiler_params=pltpu.CompilerParams(vmem_limit_bytes=2 * MIB),
    )(
        core,
        in_hbm(tokens),
        in_hbm(routes.transpose(0, 2, 1)),
        in_hbm(gating.transpose(0, 2, 1)),
    )


def fetch_first(gate_weight, up_weight, after):
    def kernel(gate_ref, up_ref, after_ref, out_ref, done_ref, sems):
        done_ref[...] = jnp.zeros_like(done_ref)
        run_copies(
            [
                pltpu.make_async_copy(
                    (gate_ref, up_ref)[j % 2].at[j // 2], out_ref.at[j], sems.at[j]
                )
                for j in range(AHEAD)
            ]
        )

    shape = (AHEAD,) + gate_weight.shape[1:]
    return pl.pallas_call(
        kernel,
        in_specs=[HBM_SPEC, HBM_SPEC, HBM_SPEC],
        out_specs=(VMEM_SPEC, VMEM_SPEC),
        out_shape=(pltpu.VMEM(shape, gate_weight.dtype), DONE),
        scratch_shapes=[pltpu.SemaphoreType.DMA((AHEAD,))],
        compiler_params=pltpu.CompilerParams(vmem_limit_bytes=MIB),
        cost_estimate=pl.CostEstimate(
            flops=0, bytes_accessed=2 * AHEAD * gate_weight[0].size, transcendentals=0
        ),
    )(in_hbm(gate_weight), in_hbm(up_weight), in_vmem(after))


def fetch_part(weight, lower, upper, after):
    def kernel(weight_ref, after_ref, out_ref, done_ref, sems):
        done_ref[...] = jnp.zeros_like(done_ref)
        run_copies(
            [
                pltpu.make_async_copy(weight_ref.at[lower + e], out_ref.at[e], sems.at[e])
                for e in range(upper - lower)
            ]
        )

    return pl.pallas_call(
        kernel,
        in_specs=[HBM_SPEC, HBM_SPEC],
        out_specs=(VMEM_SPEC, VMEM_SPEC),
        out_shape=(pltpu.VMEM((upper - lower,) + weight.shape[1:], weight.dtype), DONE),
        scratch_shapes=[pltpu.SemaphoreType.DMA((upper - lower,))],
        compiler_params=pltpu.CompilerParams(vmem_limit_bytes=MIB),
        cost_estimate=pl.CostEstimate(
            flops=0, bytes_accessed=2 * (upper - lower) * weight[0].size, transcendentals=0
        ),
    )(in_hbm(weight), in_vmem(after))


def add(out_rows, *terms, after=None):
    extra = [] if after is None else [in_vmem(after)]

    def kernel(*refs):
        total = None
        for ref, (_, lower) in zip(refs, terms):
            value = ref[lower : lower + out_rows, :].astype(jnp.float32)
            total = value if total is None else total + value
        refs[-1][...] = total.astype(jnp.bfloat16)

    return pl.pallas_call(
        kernel,
        in_specs=[VMEM_SPEC] * len(terms) + [HBM_SPEC] * len(extra),
        out_specs=VMEM_SPEC,
        out_shape=pltpu.VMEM((out_rows, terms[0][0].shape[1]), jnp.bfloat16),
        compiler_params=pltpu.CompilerParams(vmem_limit_bytes=2 * MIB),
        cost_estimate=SMALL,
    )(*[in_vmem(value) for value, _ in terms], *extra)


def stack(parts, after):
    heights = [part.shape[0] for part in parts]

    def kernel(*refs):
        base = 0
        for ref, height in zip(refs, heights):
            refs[-1][base : base + height, :] = ref[...]
            base += height

    return pl.pallas_call(
        kernel,
        in_specs=[VMEM_SPEC] * len(parts) + [HBM_SPEC],
        out_specs=VMEM_SPEC,
        out_shape=pltpu.VMEM((sum(heights), parts[0].shape[1]), parts[0].dtype),
        compiler_params=pltpu.CompilerParams(vmem_limit_bytes=2 * MIB),
        cost_estimate=SMALL,
    )(*[in_vmem(part) for part in parts], in_vmem(after))


def expert_kernel(
    topk,
    cap_cold,
    cap_hot,
    place_ref,
    mine_ref,
    theirs_ref,
    gate_ref,
    up_ref,
    down_refs,
    first_ref,
    keep_near,
    keep_far,
    send_near,
    send_far,
    rank_rows,
    weight_rows,
    counts,
    gathered,
    returned,
    hot_rows,
    hot_seen,
    ring,
    sems,
):
    experts_here, features, hidden = gate_ref.shape
    rows = mine_ref.shape[0]
    half = features // 2
    cold_rows = experts_here * cap_cold
    blocks = 2 * experts_here
    core = place_ref[1]
    my_half = pl.ds(pl.multiple_of(core * half, 128), half)
    other_half = pl.ds(pl.multiple_of((1 - core) * half, 128), half)

    def slot_of(block):
        return lax.rem(block, RING)

    def refill(block, which):
        source = (gate_ref, up_ref)[which]
        slot = slot_of(block)
        return pltpu.make_async_copy(
            source.at[lax.div(block, 2)], ring.at[slot], sems.at[slot]
        )

    for block in range(AHEAD, min(AHEAD + RING, blocks)):
        refill(block, block % 2).start()

    def gather(selector, target):
        target[:, my_half] = jnp.dot(
            selector, mine_ref[:, :half], preferred_element_type=jnp.float32
        ).astype(jnp.bfloat16)
        target[:, other_half] = jnp.dot(
            selector, theirs_ref[:, :half], preferred_element_type=jnp.float32
        ).astype(jnp.bfloat16)

    def pick(expert, count):
        slots = lax.broadcasted_iota(jnp.int32, (count, rows), 0).astype(jnp.float32)
        return jnp.where(rank_rows[pl.ds(expert, 1), :] == slots, 1.0, 0.0)

    hot_seen[0] = -1
    meta = mine_ref[:, half:].astype(jnp.float32)
    lane = lax.broadcasted_iota(jnp.int32, (rows, 128), 1)
    wanted = (place_ref[0] * experts_here + lane).astype(jnp.float32)
    member = jnp.zeros((rows, 128), jnp.float32)
    weight = jnp.zeros((rows, 128), jnp.float32)
    for k in range(topk):
        gate = (
            meta[:, topk + k : topk + k + 1]
            + meta[:, 2 * topk + k : 2 * topk + k + 1]
            + meta[:, 3 * topk + k : 3 * topk + k + 1]
        )
        hit = (meta[:, k : k + 1] == wanted) & (lane < experts_here)
        member = member + jnp.where(hit, 1.0, 0.0)
        weight = weight + jnp.where(hit, gate, 0.0)
    earlier = lax.broadcasted_iota(jnp.int32, (rows, rows), 1) < lax.broadcasted_iota(
        jnp.int32, (rows, rows), 0
    )
    rank = jnp.dot(
        jnp.where(earlier, 1.0, 0.0).astype(jnp.bfloat16),
        member.astype(jnp.bfloat16),
        preferred_element_type=jnp.float32,
    )
    rank_rows[...] = jnp.where(member > 0.0, rank, -1.0).T
    weight_rows[...] = weight.T
    totals = jnp.sum(member, axis=0, keepdims=True)
    for e in range(experts_here):
        counts[e] = totals[0, e].astype(jnp.int32)
    selector = jnp.concatenate([pick(e, cap_cold) for e in range(experts_here)], axis=0)
    gather(selector.astype(jnp.bfloat16), gathered)

    def project(expert, which, row_data, fetched):
        if fetched:
            return jnp.dot(row_data, first_ref[which], preferred_element_type=jnp.float32)
        block = 2 * expert + which
        refill(block, which).wait()
        value = jnp.dot(row_data, ring[slot_of(block)], preferred_element_type=jnp.float32)

        @pl.when(block + RING < blocks)
        def _():
            refill(block + RING, which).start()

        return value

    def visit(expert, fetched, down_ref, base):
        def forward(row_data, weight_column):
            gate_proj = project(expert, 0, row_data, fetched)
            up_proj = project(expert, 1, row_data, fetched)
            active = (jax.nn.silu(gate_proj) * up_proj).astype(jnp.bfloat16)
            partial = jnp.dot(
                active, down_ref[expert - base], preferred_element_type=jnp.float32
            )
            return (partial * weight_column).astype(jnp.bfloat16)

        first_row = expert * cap_cold
        if not isinstance(first_row, int):
            first_row = pl.multiple_of(first_row, cap_cold)
        block = pl.ds(first_row, cap_cold)
        is_hot = counts[expert] > cap_cold

        @pl.when(jnp.logical_not(is_hot))
        def _():
            weight_column = jnp.sum(
                pick(expert, cap_cold) * weight_rows[pl.ds(expert, 1), :],
                axis=1,
                keepdims=True,
            )
            returned[block, :] = forward(gathered[block, :], weight_column)

        @pl.when(is_hot)
        def _():
            selector = pick(expert, cap_hot)
            gather(selector.astype(jnp.bfloat16), hot_rows)
            weight_column = jnp.sum(
                selector * weight_rows[pl.ds(expert, 1), :], axis=1, keepdims=True
            )
            returned[block, :] = jnp.zeros((cap_cold, features), jnp.bfloat16)
            returned[cold_rows:, :] = forward(hot_rows[...], weight_column)
            hot_seen[0] = expert

    visit(0, True, down_refs[0], 0)
    base = 0
    for down_ref in down_refs:

        @pl.loop(max(base, 1), base + down_ref.shape[0])
        def _(expert):
            visit(expert, False, down_ref, base)

        base += down_ref.shape[0]

    near = rows // 2
    spread = jnp.concatenate(
        [pick(e, cap_cold) for e in range(experts_here)], axis=0
    ).T.astype(jnp.bfloat16)

    def combine(spread, slots):
        for start in range(0, half, half // 2):
            for core_of, near_ref, far_ref in (
                (core, keep_near, keep_far),
                (1 - core, send_near, send_far),
            ):
                columns = pl.ds(pl.multiple_of(core_of * half + start, 128), half // 2)
                value = jnp.dot(
                    spread, returned[:slots, columns], preferred_element_type=jnp.float32
                ).astype(jnp.bfloat16)
                near_ref[:, start : start + half // 2] = value[:near]
                far_ref[:, start : start + half // 2] = value[near:]

    @pl.when(hot_seen[0] < 0)
    def _():
        combine(spread, cold_rows)

    @pl.when(hot_seen[0] >= 0)
    def _():
        hot_spread = pick(hot_seen[0], cap_hot).T.astype(jnp.bfloat16)
        combine(jnp.concatenate([spread, hot_spread], axis=1), cold_rows + cap_hot)


def run_experts(
    place, mine, theirs, gate_weight, up_weight, down_parts, first, topk, cap_cold, cap_hot
):
    rows = mine.shape[0]
    experts_here, features, hidden = gate_weight.shape
    half = features // 2
    out = pltpu.VMEM((rows // 2, half), jnp.bfloat16)
    return pl.pallas_call(
        functools.partial(expert_kernel, topk, cap_cold, cap_hot),
        in_specs=[
            pl.BlockSpec(memory_space=pltpu.SMEM),
            VMEM_SPEC,
            VMEM_SPEC,
            HBM_SPEC,
            HBM_SPEC,
            [VMEM_SPEC] * len(down_parts),
            VMEM_SPEC,
        ],
        out_specs=[VMEM_SPEC] * 4,
        out_shape=[out] * 4,
        scratch_shapes=[
            pltpu.VMEM((128, rows), jnp.float32),
            pltpu.VMEM((128, rows), jnp.float32),
            pltpu.SMEM((experts_here,), jnp.int32),
            pltpu.VMEM((experts_here * cap_cold, features), jnp.bfloat16),
            pltpu.VMEM((experts_here * cap_cold + cap_hot, features), jnp.bfloat16),
            pltpu.VMEM((cap_hot, features), jnp.bfloat16),
            pltpu.SMEM((1,), jnp.int32),
            pltpu.VMEM((RING, features, hidden), jnp.bfloat16),
            pltpu.SemaphoreType.DMA((RING,)),
        ],
        compiler_params=pltpu.CompilerParams(vmem_limit_bytes=24 * MIB),
        cost_estimate=pl.CostEstimate(
            flops=6 * rows * features * hidden,
            bytes_accessed=4 * experts_here * features * hidden,
            transcendentals=0,
        ),
    )(
        place,
        in_vmem(mine),
        in_vmem(theirs),
        in_hbm(gate_weight),
        in_hbm(up_weight),
        [in_vmem(part) for part in down_parts],
        in_vmem(first),
    )


def local(tokens, routes, gating, gate_weight, up_weight, down_weight):
    step_count, tok_dev, features = tokens.shape
    topk = routes.shape[2]
    experts_here = gate_weight.shape[0]
    devices = lax.axis_size("expert")
    half = features // 2
    rows = step_count * tok_dev
    core = lax.axis_index("tensor").astype(jnp.int32)

    def across(value):
        return lax.ppermute(value, "tensor", [(0, 1), (1, 0)])

    def trade(value, k):
        return lax.ppermute(value, "expert", [(i, i ^ k) for i in range(devices)])

    own = prepare(core[None], tokens, routes, gating)
    there2 = trade(own, 4)
    there1 = trade(own, 2)
    beside0 = trade(own, 1)
    down_a, _ = fetch_part(down_weight, 0, 4, own)
    there3 = trade(there2, 2)
    beside12 = trade(jnp.concatenate([there1, there2]), 1)
    down_b, fetched_b = fetch_part(down_weight, 4, 7, there1)
    there3 = stack([there3], fetched_b)
    beside3 = trade(there3, 1)
    first, fetched_first = fetch_first(gate_weight, up_weight, there3)
    column = jnp.concatenate([own, there1, there2, there3])
    beside = stack([beside0, beside12, beside3], fetched_first)
    down_c, _ = fetch_part(down_weight, 7, 8, beside3)
    mine = jnp.concatenate([column, beside])
    theirs = jnp.concatenate([across(column), across(beside)])

    place = jnp.stack([lax.axis_index("expert").astype(jnp.int32), core])
    keep_near, keep_far, send_near, send_far = run_experts(
        place,
        mine,
        theirs,
        gate_weight,
        up_weight,
        [down_a, down_b, down_c],
        first,
        topk,
        step_count * devices * 2,
        step_count * devices * (tok_dev * 5 // 8),
    )

    other_far = across(send_far)
    other_near = across(send_near)
    from3 = trade(add(rows, (keep_far, 3 * rows), (other_far, 3 * rows)), 1)
    from2 = trade(add(rows, (keep_far, 2 * rows), (other_far, 2 * rows)), 1)
    sum3 = add(rows, (keep_near, 3 * rows), (other_near, 3 * rows), (from3, 0))
    from01 = trade(add(2 * rows, (keep_far, 0), (other_far, 0), after=sum3), 1)
    on3 = trade(sum3, 2)
    sum2 = add(rows, (keep_near, 2 * rows), (other_near, 2 * rows), (from2, 0), (on3, 0))
    on2 = trade(sum2, 4)
    sum1 = add(rows, (keep_near, rows), (other_near, rows), (from01, rows))
    on1 = trade(sum1, 2)
    total = on2.astype(jnp.float32)
    for term in (on1, from01[:rows], other_near[:rows], keep_near[:rows]):
        total = total + term.astype(jnp.float32)
    return total.astype(jnp.bfloat16).reshape(step_count, tok_dev, half)


def expert_block(received, w_gate, w_up, w_down):
    gate_proj = jnp.einsum("nemd,edf->nemf", received, w_gate, preferred_element_type=jnp.float32)
    up_proj = jnp.einsum("nemd,edf->nemf", received, w_up, preferred_element_type=jnp.float32)
    active = (jax.nn.silu(gate_proj) * up_proj).astype(jnp.bfloat16)
    return jnp.einsum("nemf,efd->nemd", active, w_down, preferred_element_type=jnp.float32).astype(
        jnp.bfloat16
    )


def pair_ranks(flat_ids):
    pair_count = flat_ids.shape[0]
    positions = jnp.arange(pair_count, dtype=jnp.int32)
    earlier = (flat_ids[:, None] == flat_ids[None, :]) & (positions[None, :] < positions[:, None])
    return jnp.sum(earlier.astype(jnp.int32), axis=1)


def pack_rows(slot_of_pair, slot_count, topk, row_data):
    slot_ids = jnp.arange(slot_count, dtype=jnp.int32)
    hits = (slot_ids[:, None] == slot_of_pair[None, :]).reshape(slot_count, -1, topk)
    selector = jnp.any(hits, axis=2).astype(jnp.bfloat16)
    return jnp.dot(selector, row_data, preferred_element_type=jnp.float32).astype(jnp.bfloat16)


def local_by_slots(tokens, routes, gating, gate_weight, up_weight, down_weight):
    step_count, tok_dev, feature_count = tokens.shape
    topk = routes.shape[2]
    experts_here = gate_weight.shape[0]
    device_count = lax.axis_size("expert")
    experts = experts_here * device_count
    hot_cap = tok_dev * 5 // 8
    outputs = []
    for step_index in range(step_count):
        token_rows = tokens[step_index]
        flat_ids = routes[step_index].reshape(-1)
        ranks = pair_ranks(flat_ids)
        send_slot = flat_ids * hot_cap + ranks
        send_buffer = pack_rows(send_slot, experts * hot_cap, topk, token_rows).reshape(
            device_count, experts_here, hot_cap, token_rows.shape[1]
        )
        results = expert_block(
            lax.all_to_all(send_buffer, "expert", split_axis=0, concat_axis=0, tiled=True),
            gate_weight,
            up_weight,
            down_weight,
        )
        returned = lax.all_to_all(
            results, "expert", split_axis=0, concat_axis=0, tiled=True
        ).reshape(experts * hot_cap, feature_count)
        pair_rows = returned[send_slot]
        weighted = (
            pair_rows.astype(jnp.float32).reshape(tok_dev, topk, feature_count)
            * gating[step_index][:, :, None]
        )
        running = jnp.sum(weighted, axis=1)
        outputs.append(
            lax.psum_scatter(running, "tensor", scatter_dimension=1, tiled=True).astype(
                jnp.bfloat16
            )
        )
    return jnp.stack(outputs)


def solution(mesh):
    body = local if mesh.shape["expert"] == 8 else local_by_slots
    in_specs = (
        P(None, ("groups", "expert"), None),
        P(None, ("groups", "expert"), None),
        P(None, ("groups", "expert"), None),
        P("expert", None, "tensor"),
        P("expert", None, "tensor"),
        P("expert", "tensor", None),
    )
    out_specs = P(None, ("groups", "expert"), "tensor")
    return jax.shard_map(body, mesh=mesh, in_specs=in_specs, out_specs=out_specs, check_vma=False)
```

```python
import functools

import jax
import jax.numpy as jnp
from jax import lax
from jax.experimental import pallas as pl
from jax.experimental.pallas import tpu as pltpu
from jax.sharding import PartitionSpec as P

META = 128
RING = 6
FETCHED = (4, 6)
MIB = 1024 * 1024


def in_vmem(value):
    return pltpu.with_memory_space_constraint(value, pltpu.VMEM)


def in_hbm(value):
    return pltpu.with_memory_space_constraint(value, pltpu.HBM)


VMEM_SPEC = pl.BlockSpec(memory_space=pltpu.VMEM)
HBM_SPEC = pl.BlockSpec(memory_space=pl.ANY)
DONE = pltpu.VMEM((8, 128), jnp.float32)
SMALL = pl.CostEstimate(flops=1, bytes_accessed=1, transcendentals=0)


def run_copies(copies):
    for copy in copies:
        copy.start()
    for copy in copies:
        copy.wait()


def prepare(tokens, routes, gating):
    step_count, tok_dev, features = tokens.shape
    topk = routes.shape[2]
    half = features // 2

    def kernel(tokens_ref, routes_hbm, gating_hbm, out_ref, routes_ref, gating_ref, sems):
        columns = pl.ds(pl.multiple_of(lax.axis_index("tensor") * half, 128), half)
        copies = [
            pltpu.make_async_copy(
                tokens_ref.at[s, :, columns],
                out_ref.at[s * tok_dev : (s + 1) * tok_dev, :half],
                sems.at[s],
            )
            for s in range(step_count)
        ]
        small = [
            pltpu.make_async_copy(routes_hbm, routes_ref, sems.at[step_count]),
            pltpu.make_async_copy(gating_hbm, gating_ref, sems.at[step_count + 1]),
        ]
        for copy in small + copies:
            copy.start()
        for copy in small:
            copy.wait()
        for s in range(step_count):
            weight = gating_ref[s].T
            top = weight.astype(jnp.bfloat16)
            rest = weight - top.astype(jnp.float32)
            middle = rest.astype(jnp.bfloat16)
            low = rest - middle.astype(jnp.float32)
            parts = [
                routes_ref[s].astype(jnp.float32).T,
                top.astype(jnp.float32),
                middle.astype(jnp.float32),
                low,
                jnp.zeros((tok_dev, META - 4 * topk), jnp.float32),
            ]
            out_ref[s * tok_dev : (s + 1) * tok_dev, half:] = jnp.concatenate(
                parts, axis=1
            ).astype(jnp.bfloat16)
        for copy in copies:
            copy.wait()

    return pl.pallas_call(
        kernel,
        in_specs=[HBM_SPEC, HBM_SPEC, HBM_SPEC],
        out_specs=VMEM_SPEC,
        out_shape=pltpu.VMEM((step_count * tok_dev, half + META), jnp.bfloat16),
        scratch_shapes=[
            pltpu.VMEM((step_count, topk, tok_dev), jnp.int32),
            pltpu.VMEM((step_count, topk, tok_dev), jnp.float32),
            pltpu.SemaphoreType.DMA((step_count + 2,)),
        ],
        compiler_params=pltpu.CompilerParams(vmem_limit_bytes=2 * MIB),
    )(
        in_hbm(tokens),
        in_hbm(routes.transpose(0, 2, 1)),
        in_hbm(gating.transpose(0, 2, 1)),
    )


def fetch_part(weight, lower, upper, after):
    def kernel(weight_ref, after_ref, out_ref, done_ref, sems):
        done_ref[...] = jnp.zeros_like(done_ref)
        run_copies(
            [
                pltpu.make_async_copy(weight_ref.at[lower + e], out_ref.at[e], sems.at[e])
                for e in range(upper - lower)
            ]
        )

    return pl.pallas_call(
        kernel,
        in_specs=[HBM_SPEC, HBM_SPEC],
        out_specs=(VMEM_SPEC, VMEM_SPEC),
        out_shape=(pltpu.VMEM((upper - lower,) + weight.shape[1:], weight.dtype), DONE),
        scratch_shapes=[pltpu.SemaphoreType.DMA((upper - lower,))],
        compiler_params=pltpu.CompilerParams(vmem_limit_bytes=MIB),
        cost_estimate=pl.CostEstimate(
            flops=0, bytes_accessed=2 * (upper - lower) * weight[0].size, transcendentals=0
        ),
    )(in_hbm(weight), in_vmem(after))


def add(out_rows, *terms, after=None):
    extra = [] if after is None else [in_vmem(after)]

    def kernel(*refs):
        total = None
        for ref, (_, lower) in zip(refs, terms):
            value = ref[lower : lower + out_rows, :].astype(jnp.float32)
            total = value if total is None else total + value
        refs[-1][...] = total.astype(jnp.bfloat16)

    return pl.pallas_call(
        kernel,
        in_specs=[VMEM_SPEC] * len(terms) + [HBM_SPEC] * len(extra),
        out_specs=VMEM_SPEC,
        out_shape=pltpu.VMEM((out_rows, terms[0][0].shape[1]), jnp.bfloat16),
        compiler_params=pltpu.CompilerParams(vmem_limit_bytes=2 * MIB),
        cost_estimate=SMALL,
    )(*[in_vmem(value) for value, _ in terms], *extra)


def stack(parts, after):
    heights = [part.shape[0] for part in parts]

    def kernel(*refs):
        base = 0
        for ref, height in zip(refs, heights):
            refs[-1][base : base + height, :] = ref[...]
            base += height

    return pl.pallas_call(
        kernel,
        in_specs=[VMEM_SPEC] * len(parts) + [HBM_SPEC],
        out_specs=VMEM_SPEC,
        out_shape=pltpu.VMEM((sum(heights), parts[0].shape[1]), parts[0].dtype),
        compiler_params=pltpu.CompilerParams(vmem_limit_bytes=2 * MIB),
        cost_estimate=SMALL,
    )(*[in_vmem(part) for part in parts], in_vmem(after))


def expert_kernel(
    topk,
    cap_cold,
    cap_hot,
    mine_ref,
    theirs_ref,
    gate_ref,
    up_ref,
    down_ref_hbm,
    down_refs,
    keep_near,
    keep_far,
    send_near,
    send_far,
    rank_rows,
    weight_rows,
    counts,
    gathered,
    returned,
    hot_rows,
    hot_seen,
    ring,
    sems,
    down_ring,
    down_sems,
):
    experts_here, features, hidden = gate_ref.shape
    rows = mine_ref.shape[0]
    half = features // 2
    cold_rows = experts_here * cap_cold
    blocks = 2 * experts_here
    core = lax.axis_index("tensor")
    my_half = pl.ds(pl.multiple_of(core * half, 128), half)
    other_half = pl.ds(pl.multiple_of((1 - core) * half, 128), half)

    def slot_of(block):
        return lax.rem(block, RING)

    def refill(block, which):
        source = (gate_ref, up_ref)[which]
        slot = slot_of(block)
        return pltpu.make_async_copy(
            source.at[lax.div(block, 2)], ring.at[slot], sems.at[slot]
        )

    for block in range(min(RING, blocks)):
        refill(block, block % 2).start()

    def gather(selector, target):
        target[:, my_half] = jnp.dot(
            selector, mine_ref[:, :half], preferred_element_type=jnp.float32
        ).astype(jnp.bfloat16)
        target[:, other_half] = jnp.dot(
            selector, theirs_ref[:, :half], preferred_element_type=jnp.float32
        ).astype(jnp.bfloat16)

    def pick(expert, count):
        slots = lax.broadcasted_iota(jnp.int32, (count, rows), 0).astype(jnp.float32)
        return jnp.where(rank_rows[pl.ds(expert, 1), :] == slots, 1.0, 0.0)

    hot_seen[0] = -1
    meta = mine_ref[:, half:].astype(jnp.float32)
    lane = lax.broadcasted_iota(jnp.int32, (rows, 128), 1)
    wanted = (lax.axis_index("expert") * experts_here + lane).astype(jnp.float32)
    member = jnp.zeros((rows, 128), jnp.float32)
    weight = jnp.zeros((rows, 128), jnp.float32)
    for k in range(topk):
        gate = (
            meta[:, topk + k : topk + k + 1]
            + meta[:, 2 * topk + k : 2 * topk + k + 1]
            + meta[:, 3 * topk + k : 3 * topk + k + 1]
        )
        hit = (meta[:, k : k + 1] == wanted) & (lane < experts_here)
        member = member + jnp.where(hit, 1.0, 0.0)
        weight = weight + jnp.where(hit, gate, 0.0)
    earlier = lax.broadcasted_iota(jnp.int32, (rows, rows), 1) < lax.broadcasted_iota(
        jnp.int32, (rows, rows), 0
    )
    rank = jnp.dot(
        jnp.where(earlier, 1.0, 0.0).astype(jnp.bfloat16),
        member.astype(jnp.bfloat16),
        preferred_element_type=jnp.float32,
    )
    rank_rows[...] = jnp.where(member > 0.0, rank, -1.0).T
    weight_rows[...] = weight.T
    totals = jnp.sum(member, axis=0, keepdims=True)
    for e in range(experts_here):
        counts[e] = totals[0, e].astype(jnp.int32)
    selector = jnp.concatenate([pick(e, cap_cold) for e in range(experts_here)], axis=0)
    gather(selector.astype(jnp.bfloat16), gathered.at[:cold_rows])

    def stream(expert):
        place = expert - FETCHED[1]
        return pltpu.make_async_copy(
            down_ref_hbm.at[expert], down_ring.at[place], down_sems.at[place]
        )

    def project(expert, which, row_data):
        block = 2 * expert + which
        refill(block, which).wait()
        value = jnp.dot(row_data, ring[slot_of(block)], preferred_element_type=jnp.float32)

        @pl.when(block + RING < blocks)
        def _():
            refill(block + RING, which).start()

        return value

    def visit(expert, down_ref, base, streamed):
        def forward(row_data, weight_column, count):
            gate_proj = project(expert, 0, row_data)[:count]
            up_proj = project(expert, 1, row_data)[:count]
            active = (jax.nn.silu(gate_proj) * up_proj).astype(jnp.bfloat16)
            if streamed:
                stream(expert).wait()
            partial = jnp.dot(
                active, down_ref[expert - base], preferred_element_type=jnp.float32
            )
            return (partial * weight_column).astype(jnp.bfloat16)

        first_row = pl.multiple_of(expert * cap_cold, cap_cold)
        block = pl.ds(first_row, cap_cold)
        wide = pl.ds(first_row, 4 * cap_cold)
        is_hot = counts[expert] > cap_cold

        @pl.when((expert + 2 >= FETCHED[1]) & (expert + 2 < experts_here))
        def _():
            stream(expert + 2).start()


        @pl.when(jnp.logical_not(is_hot))
        def _():
            weight_column = jnp.sum(
                pick(expert, cap_cold) * weight_rows[pl.ds(expert, 1), :],
                axis=1,
                keepdims=True,
            )
            returned[block, :] = forward(gathered[wide, :], weight_column, cap_cold)

        @pl.when(is_hot)
        def _():
            selector = pick(expert, cap_hot)
            gather(selector.astype(jnp.bfloat16), hot_rows)
            weight_column = jnp.sum(
                selector * weight_rows[pl.ds(expert, 1), :], axis=1, keepdims=True
            )
            returned[block, :] = jnp.zeros((cap_cold, features), jnp.bfloat16)
            returned[cold_rows:, :] = forward(hot_rows[...], weight_column, cap_hot)
            hot_seen[0] = expert

    base = 0
    for down_ref, streamed in [(ref, False) for ref in down_refs] + [(down_ring, True)]:

        @pl.loop(base, base + down_ref.shape[0])
        def _(expert):
            visit(expert, down_ref, base, streamed)

        base += down_ref.shape[0]

    near = rows // 2
    spread = jnp.concatenate(
        [pick(e, cap_cold) for e in range(experts_here)], axis=0
    ).T.astype(jnp.bfloat16)

    def combine(spread, slots):
        for start in range(0, half, half // 2):
            for core_of, near_ref, far_ref in (
                (core, keep_near, keep_far),
                (1 - core, send_near, send_far),
            ):
                columns = pl.ds(pl.multiple_of(core_of * half + start, 128), half // 2)
                value = jnp.dot(
                    spread, returned[:slots, columns], preferred_element_type=jnp.float32
                ).astype(jnp.bfloat16)
                near_ref[:, start : start + half // 2] = value[:near]
                far_ref[:, start : start + half // 2] = value[near:]

    @pl.when(hot_seen[0] < 0)
    def _():
        combine(spread, cold_rows)

    @pl.when(hot_seen[0] >= 0)
    def _():
        hot_spread = pick(hot_seen[0], cap_hot).T.astype(jnp.bfloat16)
        combine(jnp.concatenate([spread, hot_spread], axis=1), cold_rows + cap_hot)


def run_experts(
    mine, theirs, gate_weight, up_weight, down_weight, down_parts, topk, cap_cold, cap_hot
):
    rows = mine.shape[0]
    experts_here, features, hidden = gate_weight.shape
    half = features // 2
    out = pltpu.VMEM((rows // 2, half), jnp.bfloat16)
    return pl.pallas_call(
        functools.partial(expert_kernel, topk, cap_cold, cap_hot),
        in_specs=[
            VMEM_SPEC,
            VMEM_SPEC,
            HBM_SPEC,
            HBM_SPEC,
            HBM_SPEC,
            [VMEM_SPEC] * len(down_parts),
        ],
        out_specs=[VMEM_SPEC] * 4,
        out_shape=[out] * 4,
        scratch_shapes=[
            pltpu.VMEM((128, rows), jnp.float32),
            pltpu.VMEM((128, rows), jnp.float32),
            pltpu.SMEM((experts_here,), jnp.int32),
            pltpu.VMEM(((experts_here + 3) * cap_cold, features), jnp.bfloat16),
            pltpu.VMEM((experts_here * cap_cold + cap_hot, features), jnp.bfloat16),
            pltpu.VMEM((cap_hot, features), jnp.bfloat16),
            pltpu.SMEM((1,), jnp.int32),
            pltpu.VMEM((RING, features, hidden), jnp.bfloat16),
            pltpu.SemaphoreType.DMA((RING,)),
            pltpu.VMEM((experts_here - FETCHED[1], hidden, features), jnp.bfloat16),
            pltpu.SemaphoreType.DMA((experts_here - FETCHED[1],)),
        ],
        compiler_params=pltpu.CompilerParams(vmem_limit_bytes=38 * MIB),
        cost_estimate=pl.CostEstimate(
            flops=6 * rows * features * hidden,
            bytes_accessed=4 * experts_here * features * hidden,
            transcendentals=0,
        ),
    )(
        in_vmem(mine),
        in_vmem(theirs),
        in_hbm(gate_weight),
        in_hbm(up_weight),
        in_hbm(down_weight),
        [in_vmem(part) for part in down_parts],
    )


def local(tokens, routes, gating, gate_weight, up_weight, down_weight):
    step_count, tok_dev, features = tokens.shape
    topk = routes.shape[2]
    experts_here = gate_weight.shape[0]
    devices = lax.axis_size("expert")
    half = features // 2
    rows = step_count * tok_dev

    def across(value):
        return lax.ppermute(value, "tensor", [(0, 1), (1, 0)])

    def trade(value, k):
        return lax.ppermute(value, "expert", [(i, i ^ k) for i in range(devices)])

    own = prepare(tokens, routes, gating)
    there2 = trade(own, 4)
    there1 = trade(own, 2)
    beside0 = trade(own, 1)
    beside1 = trade(own, 3)
    down_a, fetched_a = fetch_part(down_weight, 0, FETCHED[0], own)
    there3 = trade(there2, 2)
    beside3 = trade(there2, 3)
    beside2 = trade(there2, 1)
    early = stack([own, there1, there2, beside0, beside1], fetched_a)
    other_early = across(early)
    down_b, fetched_b = fetch_part(down_weight, FETCHED[0], FETCHED[1], there2)
    late = stack([there3, beside2, beside3], fetched_b)
    mine = jnp.concatenate([early, late])
    theirs = jnp.concatenate([other_early, across(late)])

    keep_near, keep_far, send_near, send_far = run_experts(
        mine,
        theirs,
        gate_weight,
        up_weight,
        down_weight,
        [down_a, down_b],
        topk,
        step_count * devices * 2,
        step_count * devices * (tok_dev * 5 // 8),
    )

    other_far = across(send_far)
    other_near = across(send_near)

    def both(place, after=None):
        keep, other = (keep_near, other_near) if place < 4 else (keep_far, other_far)
        lower = (place % 4) * rows
        return add(rows, (keep, lower), (other, lower), after=after)

    from2 = trade(both(6), 1)
    from3 = trade(both(7), 3)
    from_there3 = trade(both(5), 2)
    from1 = trade(both(4, other_near), 3)
    from0 = trade(both(3), 1)
    from_there1 = trade(both(1), 2)
    far2 = 2 * rows
    sum2 = add(
        rows, (keep_near, far2), (other_near, far2), (from2, 0), (from3, 0), (from_there3, 0)
    )
    on2 = trade(sum2, 4)
    total = on2.astype(jnp.float32)
    for term in (from1, from0, from_there1, other_near[:rows], keep_near[:rows]):
        total = total + term.astype(jnp.float32)
    return total.astype(jnp.bfloat16).reshape(step_count, tok_dev, half)


def expert_block(received, w_gate, w_up, w_down):
    gate_proj = jnp.einsum("nemd,edf->nemf", received, w_gate, preferred_element_type=jnp.float32)
    up_proj = jnp.einsum("nemd,edf->nemf", received, w_up, preferred_element_type=jnp.float32)
    active = (jax.nn.silu(gate_proj) * up_proj).astype(jnp.bfloat16)
    return jnp.einsum("nemf,efd->nemd", active, w_down, preferred_element_type=jnp.float32).astype(
        jnp.bfloat16
    )


def pair_ranks(flat_ids):
    pair_count = flat_ids.shape[0]
    positions = jnp.arange(pair_count, dtype=jnp.int32)
    earlier = (flat_ids[:, None] == flat_ids[None, :]) & (positions[None, :] < positions[:, None])
    return jnp.sum(earlier.astype(jnp.int32), axis=1)


def pack_rows(slot_of_pair, slot_count, topk, row_data):
    slot_ids = jnp.arange(slot_count, dtype=jnp.int32)
    hits = (slot_ids[:, None] == slot_of_pair[None, :]).reshape(slot_count, -1, topk)
    selector = jnp.any(hits, axis=2).astype(jnp.bfloat16)
    return jnp.dot(selector, row_data, preferred_element_type=jnp.float32).astype(jnp.bfloat16)


def local_by_slots(tokens, routes, gating, gate_weight, up_weight, down_weight):
    step_count, tok_dev, feature_count = tokens.shape
    topk = routes.shape[2]
    experts_here = gate_weight.shape[0]
    device_count = lax.axis_size("expert")
    experts = experts_here * device_count
    hot_cap = tok_dev * 5 // 8
    outputs = []
    for step_index in range(step_count):
        token_rows = tokens[step_index]
        flat_ids = routes[step_index].reshape(-1)
        ranks = pair_ranks(flat_ids)
        send_slot = flat_ids * hot_cap + ranks
        send_buffer = pack_rows(send_slot, experts * hot_cap, topk, token_rows).reshape(
            device_count, experts_here, hot_cap, token_rows.shape[1]
        )
        results = expert_block(
            lax.all_to_all(send_buffer, "expert", split_axis=0, concat_axis=0, tiled=True),
            gate_weight,
            up_weight,
            down_weight,
        )
        returned = lax.all_to_all(
            results, "expert", split_axis=0, concat_axis=0, tiled=True
        ).reshape(experts * hot_cap, feature_count)
        pair_rows = returned[send_slot]
        weighted = (
            pair_rows.astype(jnp.float32).reshape(tok_dev, topk, feature_count)
            * gating[step_index][:, :, None]
        )
        running = jnp.sum(weighted, axis=1)
        outputs.append(
            lax.psum_scatter(running, "tensor", scatter_dimension=1, tiled=True).astype(
                jnp.bfloat16
            )
        )
    return jnp.stack(outputs)


def solution(mesh):
    body = local if mesh.shape["expert"] == 8 else local_by_slots
    in_specs = (
        P(None, ("groups", "expert"), None),
        P(None, ("groups", "expert"), None),
        P(None, ("groups", "expert"), None),
        P("expert", None, "tensor"),
        P("expert", None, "tensor"),
        P("expert", "tensor", None),
    )
    out_specs = P(None, ("groups", "expert"), "tensor")
    return jax.shard_map(body, mesh=mesh, in_specs=in_specs, out_specs=out_specs, check_vma=False)
```

```python
import functools

import jax
import jax.numpy as jnp
from jax import lax
from jax.experimental import pallas as pl
from jax.experimental.pallas import tpu as pltpu
from jax.sharding import PartitionSpec as P

META = 128
LOOK = 4
RING = 5
FETCHED = (4, 7)
MIB = 1024 * 1024


def in_vmem(value):
    return pltpu.with_memory_space_constraint(value, pltpu.VMEM)


def in_hbm(value):
    return pltpu.with_memory_space_constraint(value, pltpu.HBM)


VMEM_SPEC = pl.BlockSpec(memory_space=pltpu.VMEM)
HBM_SPEC = pl.BlockSpec(memory_space=pl.ANY)
DONE = pltpu.VMEM((8, 128), jnp.float32)
SMALL = pl.CostEstimate(flops=1, bytes_accessed=1, transcendentals=0)


def run_copies(copies):
    for copy in copies:
        copy.start()
    for copy in copies:
        copy.wait()


def prepare(tokens, routes, gating):
    step_count, tok_dev, features = tokens.shape
    topk = routes.shape[2]
    half = features // 2

    def kernel(tokens_ref, routes_hbm, gating_hbm, out_ref, routes_ref, gating_ref, sems):
        columns = pl.ds(pl.multiple_of(lax.axis_index("tensor") * half, 128), half)
        copies = [
            pltpu.make_async_copy(
                tokens_ref.at[s, :, columns],
                out_ref.at[s * tok_dev : (s + 1) * tok_dev, :half],
                sems.at[s],
            )
            for s in range(step_count)
        ]
        small = [
            pltpu.make_async_copy(routes_hbm, routes_ref, sems.at[step_count]),
            pltpu.make_async_copy(gating_hbm, gating_ref, sems.at[step_count + 1]),
        ]
        for copy in small + copies:
            copy.start()
        for copy in small:
            copy.wait()
        for s in range(step_count):
            weight = gating_ref[s].T
            top = weight.astype(jnp.bfloat16)
            rest = weight - top.astype(jnp.float32)
            middle = rest.astype(jnp.bfloat16)
            low = rest - middle.astype(jnp.float32)
            parts = [
                routes_ref[s].astype(jnp.float32).T,
                top.astype(jnp.float32),
                middle.astype(jnp.float32),
                low,
                jnp.zeros((tok_dev, META - 4 * topk), jnp.float32),
            ]
            out_ref[s * tok_dev : (s + 1) * tok_dev, half:] = jnp.concatenate(
                parts, axis=1
            ).astype(jnp.bfloat16)
        for copy in copies:
            copy.wait()

    return pl.pallas_call(
        kernel,
        in_specs=[HBM_SPEC, HBM_SPEC, HBM_SPEC],
        out_specs=VMEM_SPEC,
        out_shape=pltpu.VMEM((step_count * tok_dev, half + META), jnp.bfloat16),
        scratch_shapes=[
            pltpu.VMEM((step_count, topk, tok_dev), jnp.int32),
            pltpu.VMEM((step_count, topk, tok_dev), jnp.float32),
            pltpu.SemaphoreType.DMA((step_count + 2,)),
        ],
        compiler_params=pltpu.CompilerParams(vmem_limit_bytes=2 * MIB),
    )(
        in_hbm(tokens),
        in_hbm(routes.transpose(0, 2, 1)),
        in_hbm(gating.transpose(0, 2, 1)),
    )


def fetch_part(weight, lower, upper, after):
    def kernel(weight_ref, after_ref, out_ref, done_ref, sems):
        done_ref[...] = jnp.zeros_like(done_ref)
        run_copies(
            [
                pltpu.make_async_copy(weight_ref.at[lower + e], out_ref.at[e], sems.at[e])
                for e in range(upper - lower)
            ]
        )

    return pl.pallas_call(
        kernel,
        in_specs=[HBM_SPEC, HBM_SPEC],
        out_specs=(VMEM_SPEC, VMEM_SPEC),
        out_shape=(pltpu.VMEM((upper - lower,) + weight.shape[1:], weight.dtype), DONE),
        scratch_shapes=[pltpu.SemaphoreType.DMA((upper - lower,))],
        compiler_params=pltpu.CompilerParams(vmem_limit_bytes=MIB),
        cost_estimate=pl.CostEstimate(
            flops=0, bytes_accessed=2 * (upper - lower) * weight[0].size, transcendentals=0
        ),
    )(in_hbm(weight), in_vmem(after))


def add(out_rows, *terms, after=None):
    extra = [] if after is None else [in_vmem(after)]

    def kernel(*refs):
        total = None
        for ref, (_, lower) in zip(refs, terms):
            value = ref[lower : lower + out_rows, :].astype(jnp.float32)
            total = value if total is None else total + value
        refs[-1][...] = total.astype(jnp.bfloat16)

    return pl.pallas_call(
        kernel,
        in_specs=[VMEM_SPEC] * len(terms) + [HBM_SPEC] * len(extra),
        out_specs=VMEM_SPEC,
        out_shape=pltpu.VMEM((out_rows, terms[0][0].shape[1]), jnp.bfloat16),
        compiler_params=pltpu.CompilerParams(vmem_limit_bytes=2 * MIB),
        cost_estimate=SMALL,
    )(*[in_vmem(value) for value, _ in terms], *extra)


def stack(parts, after):
    heights = [part.shape[0] for part in parts]

    def kernel(*refs):
        base = 0
        for ref, height in zip(refs, heights):
            refs[-1][base : base + height, :] = ref[...]
            base += height

    return pl.pallas_call(
        kernel,
        in_specs=[VMEM_SPEC] * len(parts) + [HBM_SPEC],
        out_specs=VMEM_SPEC,
        out_shape=pltpu.VMEM((sum(heights), parts[0].shape[1]), parts[0].dtype),
        compiler_params=pltpu.CompilerParams(vmem_limit_bytes=2 * MIB),
        cost_estimate=SMALL,
    )(*[in_vmem(part) for part in parts], in_vmem(after))


def expert_kernel(
    topk,
    cap_cold,
    cap_hot,
    mine_ref,
    theirs_ref,
    gate_ref,
    up_ref,
    down_ref_hbm,
    down_refs,
    keep_near,
    keep_far,
    send_near,
    send_far,
    rank_rows,
    weight_rows,
    counts,
    gathered,
    returned,
    hot_rows,
    hot_seen,
    ring,
    sems,
    down_ring,
    down_sems,
):
    experts_here, features, hidden = gate_ref.shape
    rows = mine_ref.shape[0]
    half = features // 2
    cold_rows = experts_here * cap_cold
    blocks = 2 * experts_here
    core = lax.axis_index("tensor")
    my_half = pl.ds(pl.multiple_of(core * half, 128), half)
    other_half = pl.ds(pl.multiple_of((1 - core) * half, 128), half)

    def slot_of(block):
        return lax.rem(block, RING)

    def refill(block, which):
        source = (gate_ref, up_ref)[which]
        slot = slot_of(block)
        return pltpu.make_async_copy(
            source.at[lax.div(block, 2)], ring.at[slot], sems.at[slot]
        )

    for block in range(2):
        refill(block, block % 2).start()

    def gather(selector, target):
        target[:, my_half] = jnp.dot(
            selector, mine_ref[:, :half], preferred_element_type=jnp.float32
        ).astype(jnp.bfloat16)
        target[:, other_half] = jnp.dot(
            selector, theirs_ref[:, :half], preferred_element_type=jnp.float32
        ).astype(jnp.bfloat16)

    def pick(expert, count):
        slots = lax.broadcasted_iota(jnp.int32, (count, rows), 0).astype(jnp.float32)
        return jnp.where(rank_rows[pl.ds(expert, 1), :] == slots, 1.0, 0.0)

    hot_seen[0] = -1
    meta = mine_ref[:, half:].astype(jnp.float32)
    lane = lax.broadcasted_iota(jnp.int32, (rows, 128), 1)
    wanted = (lax.axis_index("expert") * experts_here + lane).astype(jnp.float32)
    member = jnp.zeros((rows, 128), jnp.float32)
    weight = jnp.zeros((rows, 128), jnp.float32)
    for k in range(topk):
        gate = (
            meta[:, topk + k : topk + k + 1]
            + meta[:, 2 * topk + k : 2 * topk + k + 1]
            + meta[:, 3 * topk + k : 3 * topk + k + 1]
        )
        hit = (meta[:, k : k + 1] == wanted) & (lane < experts_here)
        member = member + jnp.where(hit, 1.0, 0.0)
        weight = weight + jnp.where(hit, gate, 0.0)
    earlier = lax.broadcasted_iota(jnp.int32, (rows, rows), 1) < lax.broadcasted_iota(
        jnp.int32, (rows, rows), 0
    )
    rank = jnp.dot(
        jnp.where(earlier, 1.0, 0.0).astype(jnp.bfloat16),
        member.astype(jnp.bfloat16),
        preferred_element_type=jnp.float32,
    )
    rank_rows[...] = jnp.where(member > 0.0, rank, -1.0).T
    weight_rows[...] = weight.T
    totals = jnp.sum(member, axis=0, keepdims=True)
    for e in range(experts_here):
        counts[e] = totals[0, e].astype(jnp.int32)
    selector = jnp.concatenate([pick(e, cap_cold) for e in range(experts_here)], axis=0)
    gather(selector.astype(jnp.bfloat16), gathered.at[:cold_rows])

    for block in range(2, min(LOOK, blocks)):
        refill(block, block % 2).start()

    def stream(expert):
        place = expert - FETCHED[1]
        return pltpu.make_async_copy(
            down_ref_hbm.at[expert], down_ring.at[place], down_sems.at[place]
        )

    def project(expert, which, row_data):
        block = 2 * expert + which
        refill(block, which).wait()

        @pl.when(block + LOOK < blocks)
        def _():
            refill(block + LOOK, (which + LOOK) % 2).start()

        value = jnp.dot(row_data, ring[slot_of(block)], preferred_element_type=jnp.float32)
        return value

    def visit(expert, down_ref, base, streamed):
        def forward(row_data, weight_column, count):
            gate_proj = project(expert, 0, row_data)[:count]
            up_proj = project(expert, 1, row_data)[:count]
            active = (jax.nn.silu(gate_proj) * up_proj).astype(jnp.bfloat16)
            if streamed:
                stream(expert).wait()
            partial = jnp.dot(
                active, down_ref[expert - base], preferred_element_type=jnp.float32
            )
            return (partial * weight_column).astype(jnp.bfloat16)

        first_row = pl.multiple_of(expert * cap_cold, cap_cold)
        block = pl.ds(first_row, cap_cold)
        wide = pl.ds(first_row, 4 * cap_cold)
        is_hot = counts[expert] > cap_cold

        @pl.when((expert + 2 >= FETCHED[1]) & (expert + 2 < experts_here))
        def _():
            stream(expert + 2).start()


        @pl.when(jnp.logical_not(is_hot))
        def _():
            weight_column = jnp.sum(
                pick(expert, cap_cold) * weight_rows[pl.ds(expert, 1), :],
                axis=1,
                keepdims=True,
            )
            returned[block, :] = forward(gathered[wide, :], weight_column, cap_cold)

        @pl.when(is_hot)
        def _():
            selector = pick(expert, cap_hot)
            gather(selector.astype(jnp.bfloat16), hot_rows)
            weight_column = jnp.sum(
                selector * weight_rows[pl.ds(expert, 1), :], axis=1, keepdims=True
            )
            returned[block, :] = jnp.zeros((cap_cold, features), jnp.bfloat16)
            returned[cold_rows:, :] = forward(hot_rows[...], weight_column, cap_hot)
            hot_seen[0] = expert

    base = 0
    for down_ref, streamed in [(ref, False) for ref in down_refs] + [(down_ring, True)]:

        @pl.loop(base, base + down_ref.shape[0])
        def _(expert):
            visit(expert, down_ref, base, streamed)

        base += down_ref.shape[0]

    near = rows // 2
    spread = jnp.concatenate(
        [pick(e, cap_cold) for e in range(experts_here)], axis=0
    ).T.astype(jnp.bfloat16)

    def combine(spread, slots):
        for start in range(0, half, half // 2):
            for core_of, near_ref, far_ref in (
                (core, keep_near, keep_far),
                (1 - core, send_near, send_far),
            ):
                columns = pl.ds(pl.multiple_of(core_of * half + start, 128), half // 2)
                value = jnp.dot(
                    spread, returned[:slots, columns], preferred_element_type=jnp.float32
                ).astype(jnp.bfloat16)
                near_ref[:, start : start + half // 2] = value[:near]
                far_ref[:, start : start + half // 2] = value[near:]

    @pl.when(hot_seen[0] < 0)
    def _():
        combine(spread, cold_rows)

    @pl.when(hot_seen[0] >= 0)
    def _():
        hot_spread = pick(hot_seen[0], cap_hot).T.astype(jnp.bfloat16)
        combine(jnp.concatenate([spread, hot_spread], axis=1), cold_rows + cap_hot)


def run_experts(
    mine, theirs, gate_weight, up_weight, down_weight, down_parts, topk, cap_cold, cap_hot
):
    rows = mine.shape[0]
    experts_here, features, hidden = gate_weight.shape
    half = features // 2
    out = pltpu.VMEM((rows // 2, half), jnp.bfloat16)
    return pl.pallas_call(
        functools.partial(expert_kernel, topk, cap_cold, cap_hot),
        in_specs=[
            VMEM_SPEC,
            VMEM_SPEC,
            HBM_SPEC,
            HBM_SPEC,
            HBM_SPEC,
            [VMEM_SPEC] * len(down_parts),
        ],
        out_specs=[VMEM_SPEC] * 4,
        out_shape=[out] * 4,
        scratch_shapes=[
            pltpu.VMEM((128, rows), jnp.float32),
            pltpu.VMEM((128, rows), jnp.float32),
            pltpu.SMEM((experts_here,), jnp.int32),
            pltpu.VMEM(((experts_here + 3) * cap_cold, features), jnp.bfloat16),
            pltpu.VMEM((experts_here * cap_cold + cap_hot, features), jnp.bfloat16),
            pltpu.VMEM((cap_hot, features), jnp.bfloat16),
            pltpu.SMEM((1,), jnp.int32),
            pltpu.VMEM((RING, features, hidden), jnp.bfloat16),
            pltpu.SemaphoreType.DMA((RING,)),
            pltpu.VMEM((experts_here - FETCHED[1], hidden, features), jnp.bfloat16),
            pltpu.SemaphoreType.DMA((experts_here - FETCHED[1],)),
        ],
        compiler_params=pltpu.CompilerParams(vmem_limit_bytes=33 * MIB),
        cost_estimate=pl.CostEstimate(
            flops=6 * rows * features * hidden,
            bytes_accessed=4 * experts_here * features * hidden,
            transcendentals=0,
        ),
    )(
        in_vmem(mine),
        in_vmem(theirs),
        in_hbm(gate_weight),
        in_hbm(up_weight),
        in_hbm(down_weight),
        [in_vmem(part) for part in down_parts],
    )


def local(tokens, routes, gating, gate_weight, up_weight, down_weight):
    step_count, tok_dev, features = tokens.shape
    topk = routes.shape[2]
    experts_here = gate_weight.shape[0]
    devices = lax.axis_size("expert")
    half = features // 2
    rows = step_count * tok_dev

    def across(value):
        return lax.ppermute(value, "tensor", [(0, 1), (1, 0)])

    def trade(value, k):
        return lax.ppermute(value, "expert", [(i, i ^ k) for i in range(devices)])

    own = prepare(tokens, routes, gating)
    there2 = trade(own, 4)
    there1 = trade(own, 2)
    beside0 = trade(own, 1)
    beside1 = trade(own, 3)
    down_a, fetched_a = fetch_part(down_weight, 0, FETCHED[0], own)
    there3 = trade(there2, 2)
    beside3 = trade(there2, 3)
    beside2 = trade(there2, 1)
    early = stack([own, there1, there2, beside0, beside1], fetched_a)
    other_early = across(early)
    down_b, fetched_b = fetch_part(down_weight, FETCHED[0], FETCHED[1], there2)
    late = stack([there3, beside2, beside3], fetched_b)
    mine = jnp.concatenate([early, late])
    theirs = jnp.concatenate([other_early, across(late)])

    keep_near, keep_far, send_near, send_far = run_experts(
        mine,
        theirs,
        gate_weight,
        up_weight,
        down_weight,
        [down_a, down_b],
        topk,
        step_count * devices * 2,
        step_count * devices * (tok_dev * 5 // 8),
    )

    other_far = across(send_far)
    other_near = across(send_near)

    def both(place, after=None):
        keep, other = (keep_near, other_near) if place < 4 else (keep_far, other_far)
        lower = (place % 4) * rows
        return add(rows, (keep, lower), (other, lower), after=after)

    from2 = trade(both(6), 1)
    from3 = trade(both(7), 3)
    from_there3 = trade(both(5), 2)
    from1 = trade(both(4, other_near), 3)
    from0 = trade(both(3), 1)
    from_there1 = trade(both(1), 2)
    far2 = 2 * rows
    sum2 = add(
        rows, (keep_near, far2), (other_near, far2), (from2, 0), (from3, 0), (from_there3, 0)
    )
    on2 = trade(sum2, 4)
    total = on2.astype(jnp.float32)
    for term in (from1, from0, from_there1, other_near[:rows], keep_near[:rows]):
        total = total + term.astype(jnp.float32)
    return total.astype(jnp.bfloat16).reshape(step_count, tok_dev, half)


def expert_block(received, w_gate, w_up, w_down):
    gate_proj = jnp.einsum("nemd,edf->nemf", received, w_gate, preferred_element_type=jnp.float32)
    up_proj = jnp.einsum("nemd,edf->nemf", received, w_up, preferred_element_type=jnp.float32)
    active = (jax.nn.silu(gate_proj) * up_proj).astype(jnp.bfloat16)
    return jnp.einsum("nemf,efd->nemd", active, w_down, preferred_element_type=jnp.float32).astype(
        jnp.bfloat16
    )


def pair_ranks(flat_ids):
    pair_count = flat_ids.shape[0]
    positions = jnp.arange(pair_count, dtype=jnp.int32)
    earlier = (flat_ids[:, None] == flat_ids[None, :]) & (positions[None, :] < positions[:, None])
    return jnp.sum(earlier.astype(jnp.int32), axis=1)


def pack_rows(slot_of_pair, slot_count, topk, row_data):
    slot_ids = jnp.arange(slot_count, dtype=jnp.int32)
    hits = (slot_ids[:, None] == slot_of_pair[None, :]).reshape(slot_count, -1, topk)
    selector = jnp.any(hits, axis=2).astype(jnp.bfloat16)
    return jnp.dot(selector, row_data, preferred_element_type=jnp.float32).astype(jnp.bfloat16)


def local_by_slots(tokens, routes, gating, gate_weight, up_weight, down_weight):
    step_count, tok_dev, feature_count = tokens.shape
    topk = routes.shape[2]
    experts_here = gate_weight.shape[0]
    device_count = lax.axis_size("expert")
    experts = experts_here * device_count
    hot_cap = tok_dev * 5 // 8
    outputs = []
    for step_index in range(step_count):
        token_rows = tokens[step_index]
        flat_ids = routes[step_index].reshape(-1)
        ranks = pair_ranks(flat_ids)
        send_slot = flat_ids * hot_cap + ranks
        send_buffer = pack_rows(send_slot, experts * hot_cap, topk, token_rows).reshape(
            device_count, experts_here, hot_cap, token_rows.shape[1]
        )
        results = expert_block(
            lax.all_to_all(send_buffer, "expert", split_axis=0, concat_axis=0, tiled=True),
            gate_weight,
            up_weight,
            down_weight,
        )
        returned = lax.all_to_all(
            results, "expert", split_axis=0, concat_axis=0, tiled=True
        ).reshape(experts * hot_cap, feature_count)
        pair_rows = returned[send_slot]
        weighted = (
            pair_rows.astype(jnp.float32).reshape(tok_dev, topk, feature_count)
            * gating[step_index][:, :, None]
        )
        running = jnp.sum(weighted, axis=1)
        outputs.append(
            lax.psum_scatter(running, "tensor", scatter_dimension=1, tiled=True).astype(
                jnp.bfloat16
            )
        )
    return jnp.stack(outputs)


def solution(mesh):
    body = local if mesh.shape["expert"] == 8 else local_by_slots
    in_specs = (
        P(None, ("groups", "expert"), None),
        P(None, ("groups", "expert"), None),
        P(None, ("groups", "expert"), None),
        P("expert", None, "tensor"),
        P("expert", None, "tensor"),
        P("expert", "tensor", None),
    )
    out_specs = P(None, ("groups", "expert"), "tensor")
    return jax.shard_map(body, mesh=mesh, in_specs=in_specs, out_specs=out_specs, check_vma=False)
```

```python
import functools

import jax
import jax.numpy as jnp
from jax import lax
from jax.experimental import pallas as pl
from jax.experimental.pallas import tpu as pltpu
from jax.sharding import PartitionSpec as P

META = 128
LOOK = 4
RING = 5
FETCHED = (4, 7)
MIB = 1024 * 1024


def in_vmem(value):
    return pltpu.with_memory_space_constraint(value, pltpu.VMEM)


def in_hbm(value):
    return pltpu.with_memory_space_constraint(value, pltpu.HBM)


VMEM_SPEC = pl.BlockSpec(memory_space=pltpu.VMEM)
HBM_SPEC = pl.BlockSpec(memory_space=pl.ANY)
DONE = pltpu.VMEM((8, 128), jnp.float32)
SMALL = pl.CostEstimate(flops=1, bytes_accessed=1, transcendentals=0)


def run_copies(copies):
    for copy in copies:
        copy.start()
    for copy in copies:
        copy.wait()


def prepare(tokens, routes, gating):
    step_count, tok_dev, features = tokens.shape
    topk = routes.shape[2]
    half = features // 2

    def kernel(tokens_ref, routes_hbm, gating_hbm, out_ref, routes_ref, gating_ref, sems):
        columns = pl.ds(pl.multiple_of(lax.axis_index("tensor") * half, 128), half)
        copies = [
            pltpu.make_async_copy(
                tokens_ref.at[s, :, columns],
                out_ref.at[s * tok_dev : (s + 1) * tok_dev, :half],
                sems.at[s],
            )
            for s in range(step_count)
        ]
        small = [
            pltpu.make_async_copy(routes_hbm, routes_ref, sems.at[step_count]),
            pltpu.make_async_copy(gating_hbm, gating_ref, sems.at[step_count + 1]),
        ]
        for copy in small + copies:
            copy.start()
        for copy in small:
            copy.wait()
        for s in range(step_count):
            weight = gating_ref[s].T
            top = weight.astype(jnp.bfloat16)
            rest = weight - top.astype(jnp.float32)
            middle = rest.astype(jnp.bfloat16)
            low = rest - middle.astype(jnp.float32)
            parts = [
                routes_ref[s].astype(jnp.float32).T,
                top.astype(jnp.float32),
                middle.astype(jnp.float32),
                low,
                jnp.zeros((tok_dev, META - 4 * topk), jnp.float32),
            ]
            out_ref[s * tok_dev : (s + 1) * tok_dev, half:] = jnp.concatenate(
                parts, axis=1
            ).astype(jnp.bfloat16)
        for copy in copies:
            copy.wait()

    return pl.pallas_call(
        kernel,
        in_specs=[HBM_SPEC, HBM_SPEC, HBM_SPEC],
        out_specs=VMEM_SPEC,
        out_shape=pltpu.VMEM((step_count * tok_dev, half + META), jnp.bfloat16),
        scratch_shapes=[
            pltpu.VMEM((step_count, topk, tok_dev), jnp.int32),
            pltpu.VMEM((step_count, topk, tok_dev), jnp.float32),
            pltpu.SemaphoreType.DMA((step_count + 2,)),
        ],
        compiler_params=pltpu.CompilerParams(vmem_limit_bytes=2 * MIB),
    )(
        in_hbm(tokens),
        in_hbm(routes.transpose(0, 2, 1)),
        in_hbm(gating.transpose(0, 2, 1)),
    )


def fetch_part(weight, lower, upper, after):
    def kernel(weight_ref, after_ref, out_ref, done_ref, sems):
        done_ref[...] = jnp.zeros_like(done_ref)
        run_copies(
            [
                pltpu.make_async_copy(weight_ref.at[lower + e], out_ref.at[e], sems.at[e])
                for e in range(upper - lower)
            ]
        )

    return pl.pallas_call(
        kernel,
        in_specs=[HBM_SPEC, HBM_SPEC],
        out_specs=(VMEM_SPEC, VMEM_SPEC),
        out_shape=(pltpu.VMEM((upper - lower,) + weight.shape[1:], weight.dtype), DONE),
        scratch_shapes=[pltpu.SemaphoreType.DMA((upper - lower,))],
        compiler_params=pltpu.CompilerParams(vmem_limit_bytes=MIB),
        cost_estimate=pl.CostEstimate(
            flops=0, bytes_accessed=2 * (upper - lower) * weight[0].size, transcendentals=0
        ),
    )(in_hbm(weight), in_vmem(after))


def add(out_rows, *terms, after=None):
    extra = [] if after is None else [in_vmem(after)]

    def kernel(*refs):
        total = None
        for ref, (_, lower) in zip(refs, terms):
            value = ref[lower : lower + out_rows, :].astype(jnp.float32)
            total = value if total is None else total + value
        refs[-1][...] = total.astype(jnp.bfloat16)

    return pl.pallas_call(
        kernel,
        in_specs=[VMEM_SPEC] * len(terms) + [HBM_SPEC] * len(extra),
        out_specs=VMEM_SPEC,
        out_shape=pltpu.VMEM((out_rows, terms[0][0].shape[1]), jnp.bfloat16),
        compiler_params=pltpu.CompilerParams(vmem_limit_bytes=2 * MIB),
        cost_estimate=SMALL,
    )(*[in_vmem(value) for value, _ in terms], *extra)


def stack(parts, after):
    heights = [part.shape[0] for part in parts]

    def kernel(*refs):
        base = 0
        for ref, height in zip(refs, heights):
            refs[-1][base : base + height, :] = ref[...]
            base += height

    return pl.pallas_call(
        kernel,
        in_specs=[VMEM_SPEC] * len(parts) + [HBM_SPEC],
        out_specs=VMEM_SPEC,
        out_shape=pltpu.VMEM((sum(heights), parts[0].shape[1]), parts[0].dtype),
        compiler_params=pltpu.CompilerParams(vmem_limit_bytes=2 * MIB),
        cost_estimate=SMALL,
    )(*[in_vmem(part) for part in parts], in_vmem(after))


def expert_kernel(
    topk,
    cap_cold,
    cap_hot,
    mine_ref,
    theirs_ref,
    gate_ref,
    up_ref,
    down_ref_hbm,
    down_refs,
    keep_near,
    keep_far,
    send_near,
    send_far,
    rank_rows,
    weight_rows,
    counts,
    gathered,
    returned,
    hot_rows,
    hot_seen,
    ring,
    sems,
    down_ring,
    down_sems,
):
    experts_here, features, hidden = gate_ref.shape
    rows = mine_ref.shape[0]
    half = features // 2
    cold_rows = experts_here * cap_cold
    blocks = 2 * experts_here
    core = lax.axis_index("tensor")
    my_half = pl.ds(pl.multiple_of(core * half, 128), half)
    other_half = pl.ds(pl.multiple_of((1 - core) * half, 128), half)

    def slot_of(block):
        return lax.rem(block, RING)

    def refill(block, which):
        source = (gate_ref, up_ref)[which]
        slot = slot_of(block)
        return pltpu.make_async_copy(
            source.at[lax.div(block, 2)], ring.at[slot], sems.at[slot]
        )

    for block in range(2):
        refill(block, block % 2).start()

    def gather(selector, target):
        target[:, my_half] = jnp.dot(
            selector, mine_ref[:, :half], preferred_element_type=jnp.float32
        ).astype(jnp.bfloat16)
        target[:, other_half] = jnp.dot(
            selector, theirs_ref[:, :half], preferred_element_type=jnp.float32
        ).astype(jnp.bfloat16)

    def pick(expert, count):
        slots = lax.broadcasted_iota(jnp.int32, (count, rows), 0).astype(jnp.float32)
        return jnp.where(rank_rows[pl.ds(expert, 1), :] == slots, 1.0, 0.0)

    hot_seen[0] = -1
    meta = mine_ref[:, half:].astype(jnp.float32)
    lane = lax.broadcasted_iota(jnp.int32, (rows, 128), 1)
    wanted = (lax.axis_index("expert") * experts_here + lane).astype(jnp.float32)
    member = jnp.zeros((rows, 128), jnp.float32)
    weight = jnp.zeros((rows, 128), jnp.float32)
    for k in range(topk):
        gate = (
            meta[:, topk + k : topk + k + 1]
            + meta[:, 2 * topk + k : 2 * topk + k + 1]
            + meta[:, 3 * topk + k : 3 * topk + k + 1]
        )
        hit = (meta[:, k : k + 1] == wanted) & (lane < experts_here)
        member = member + jnp.where(hit, 1.0, 0.0)
        weight = weight + jnp.where(hit, gate, 0.0)
    earlier = lax.broadcasted_iota(jnp.int32, (rows, rows), 1) < lax.broadcasted_iota(
        jnp.int32, (rows, rows), 0
    )
    rank = jnp.dot(
        jnp.where(earlier, 1.0, 0.0).astype(jnp.bfloat16),
        member.astype(jnp.bfloat16),
        preferred_element_type=jnp.float32,
    )
    rank_rows[...] = jnp.where(member > 0.0, rank, -1.0).T
    weight_rows[...] = weight.T
    totals = jnp.sum(member, axis=0, keepdims=True)
    for e in range(experts_here):
        counts[e] = totals[0, e].astype(jnp.int32)
    selector = jnp.concatenate([pick(e, cap_cold) for e in range(experts_here)], axis=0)
    gather(selector.astype(jnp.bfloat16), gathered.at[:cold_rows])

    for block in range(2, min(LOOK, blocks)):
        refill(block, block % 2).start()

    def stream(expert):
        place = expert - FETCHED[1]
        return pltpu.make_async_copy(
            down_ref_hbm.at[expert], down_ring.at[place], down_sems.at[place]
        )

    def project(expert, which, row_data):
        block = 2 * expert + which
        refill(block, which).wait()

        @pl.when(block + LOOK < blocks)
        def _():
            refill(block + LOOK, (which + LOOK) % 2).start()

        value = jnp.dot(row_data, ring[slot_of(block)], preferred_element_type=jnp.float32)
        return value

    def visit(expert, down_ref, base, streamed):
        def forward(row_data, weight_column, count):
            gate_proj = project(expert, 0, row_data)
            up_proj = project(expert, 1, row_data)
            active = (jax.nn.silu(gate_proj) * up_proj).astype(jnp.bfloat16)
            if streamed:
                stream(expert).wait()
            partial = jnp.dot(
                active, down_ref[expert - base], preferred_element_type=jnp.float32
            )
            return (partial[:count] * weight_column).astype(jnp.bfloat16)

        first_row = pl.multiple_of(expert * cap_cold, cap_cold)
        block = pl.ds(first_row, cap_cold)
        wide = pl.ds(first_row, 4 * cap_cold)
        is_hot = counts[expert] > cap_cold

        @pl.when((expert + 2 >= FETCHED[1]) & (expert + 2 < experts_here))
        def _():
            stream(expert + 2).start()


        @pl.when(jnp.logical_not(is_hot))
        def _():
            weight_column = jnp.sum(
                pick(expert, cap_cold) * weight_rows[pl.ds(expert, 1), :],
                axis=1,
                keepdims=True,
            )
            returned[block, :] = forward(gathered[wide, :], weight_column, cap_cold)

        @pl.when(is_hot)
        def _():
            selector = pick(expert, cap_hot)
            gather(selector.astype(jnp.bfloat16), hot_rows)
            weight_column = jnp.sum(
                selector * weight_rows[pl.ds(expert, 1), :], axis=1, keepdims=True
            )
            returned[block, :] = jnp.zeros((cap_cold, features), jnp.bfloat16)
            returned[cold_rows:, :] = forward(hot_rows[...], weight_column, cap_hot)
            hot_seen[0] = expert

    base = 0
    for down_ref, streamed in [(ref, False) for ref in down_refs] + [(down_ring, True)]:

        @pl.loop(base, base + down_ref.shape[0])
        def _(expert):
            visit(expert, down_ref, base, streamed)

        base += down_ref.shape[0]

    near = rows // 2
    spread = jnp.concatenate(
        [pick(e, cap_cold) for e in range(experts_here)], axis=0
    ).T.astype(jnp.bfloat16)

    def combine(spread, slots):
        for start in range(0, half, half // 2):
            for core_of, near_ref, far_ref in (
                (core, keep_near, keep_far),
                (1 - core, send_near, send_far),
            ):
                columns = pl.ds(pl.multiple_of(core_of * half + start, 128), half // 2)
                value = jnp.dot(
                    spread, returned[:slots, columns], preferred_element_type=jnp.float32
                ).astype(jnp.bfloat16)
                near_ref[:, start : start + half // 2] = value[:near]
                far_ref[:, start : start + half // 2] = value[near:]

    @pl.when(hot_seen[0] < 0)
    def _():
        combine(spread, cold_rows)

    @pl.when(hot_seen[0] >= 0)
    def _():
        hot_spread = pick(hot_seen[0], cap_hot).T.astype(jnp.bfloat16)
        combine(jnp.concatenate([spread, hot_spread], axis=1), cold_rows + cap_hot)


def run_experts(
    mine, theirs, gate_weight, up_weight, down_weight, down_parts, topk, cap_cold, cap_hot
):
    rows = mine.shape[0]
    experts_here, features, hidden = gate_weight.shape
    half = features // 2
    out = pltpu.VMEM((rows // 2, half), jnp.bfloat16)
    return pl.pallas_call(
        functools.partial(expert_kernel, topk, cap_cold, cap_hot),
        in_specs=[
            VMEM_SPEC,
            VMEM_SPEC,
            HBM_SPEC,
            HBM_SPEC,
            HBM_SPEC,
            [VMEM_SPEC] * len(down_parts),
        ],
        out_specs=[VMEM_SPEC] * 4,
        out_shape=[out] * 4,
        scratch_shapes=[
            pltpu.VMEM((128, rows), jnp.float32),
            pltpu.VMEM((128, rows), jnp.float32),
            pltpu.SMEM((experts_here,), jnp.int32),
            pltpu.VMEM(((experts_here + 3) * cap_cold, features), jnp.bfloat16),
            pltpu.VMEM((experts_here * cap_cold + cap_hot, features), jnp.bfloat16),
            pltpu.VMEM((cap_hot, features), jnp.bfloat16),
            pltpu.SMEM((1,), jnp.int32),
            pltpu.VMEM((RING, features, hidden), jnp.bfloat16),
            pltpu.SemaphoreType.DMA((RING,)),
            pltpu.VMEM((experts_here - FETCHED[1], hidden, features), jnp.bfloat16),
            pltpu.SemaphoreType.DMA((experts_here - FETCHED[1],)),
        ],
        compiler_params=pltpu.CompilerParams(vmem_limit_bytes=33 * MIB),
        cost_estimate=pl.CostEstimate(
            flops=6 * rows * features * hidden,
            bytes_accessed=4 * experts_here * features * hidden,
            transcendentals=0,
        ),
    )(
        in_vmem(mine),
        in_vmem(theirs),
        in_hbm(gate_weight),
        in_hbm(up_weight),
        in_hbm(down_weight),
        [in_vmem(part) for part in down_parts],
    )


def local(tokens, routes, gating, gate_weight, up_weight, down_weight):
    step_count, tok_dev, features = tokens.shape
    topk = routes.shape[2]
    experts_here = gate_weight.shape[0]
    devices = lax.axis_size("expert")
    half = features // 2
    rows = step_count * tok_dev

    def across(value):
        return lax.ppermute(value, "tensor", [(0, 1), (1, 0)])

    def trade(value, k):
        return lax.ppermute(value, "expert", [(i, i ^ k) for i in range(devices)])

    own = prepare(tokens, routes, gating)
    there2 = trade(own, 4)
    there1 = trade(own, 2)
    beside0 = trade(own, 1)
    beside1 = trade(own, 3)
    down_a, fetched_a = fetch_part(down_weight, 0, FETCHED[0], own)
    there3 = trade(there2, 2)
    beside3 = trade(there2, 3)
    beside2 = trade(there2, 1)
    early = stack([own, there1, there2, beside0, beside1], fetched_a)
    other_early = across(early)
    down_b, fetched_b = fetch_part(down_weight, FETCHED[0], FETCHED[1], there2)
    late = stack([there3, beside2, beside3], fetched_b)
    mine = jnp.concatenate([early, late])
    theirs = jnp.concatenate([other_early, across(late)])

    keep_near, keep_far, send_near, send_far = run_experts(
        mine,
        theirs,
        gate_weight,
        up_weight,
        down_weight,
        [down_a, down_b],
        topk,
        step_count * devices * 2,
        step_count * devices * (tok_dev * 5 // 8),
    )

    other_far = across(send_far)
    other_near = across(send_near)

    def both(place, after=None):
        keep, other = (keep_near, other_near) if place < 4 else (keep_far, other_far)
        lower = (place % 4) * rows
        return add(rows, (keep, lower), (other, lower), after=after)

    from2 = trade(both(6), 1)
    from3 = trade(both(7), 3)
    from_there3 = trade(both(5), 2)
    from1 = trade(both(4, other_near), 3)
    from0 = trade(both(3), 1)
    from_there1 = trade(both(1), 2)
    far2 = 2 * rows
    sum2 = add(
        rows, (keep_near, far2), (other_near, far2), (from2, 0), (from3, 0), (from_there3, 0)
    )
    on2 = trade(sum2, 4)
    total = on2.astype(jnp.float32)
    for term in (from1, from0, from_there1, other_near[:rows], keep_near[:rows]):
        total = total + term.astype(jnp.float32)
    return total.astype(jnp.bfloat16).reshape(step_count, tok_dev, half)


def expert_block(received, w_gate, w_up, w_down):
    gate_proj = jnp.einsum("nemd,edf->nemf", received, w_gate, preferred_element_type=jnp.float32)
    up_proj = jnp.einsum("nemd,edf->nemf", received, w_up, preferred_element_type=jnp.float32)
    active = (jax.nn.silu(gate_proj) * up_proj).astype(jnp.bfloat16)
    return jnp.einsum("nemf,efd->nemd", active, w_down, preferred_element_type=jnp.float32).astype(
        jnp.bfloat16
    )


def pair_ranks(flat_ids):
    pair_count = flat_ids.shape[0]
    positions = jnp.arange(pair_count, dtype=jnp.int32)
    earlier = (flat_ids[:, None] == flat_ids[None, :]) & (positions[None, :] < positions[:, None])
    return jnp.sum(earlier.astype(jnp.int32), axis=1)


def pack_rows(slot_of_pair, slot_count, topk, row_data):
    slot_ids = jnp.arange(slot_count, dtype=jnp.int32)
    hits = (slot_ids[:, None] == slot_of_pair[None, :]).reshape(slot_count, -1, topk)
    selector = jnp.any(hits, axis=2).astype(jnp.bfloat16)
    return jnp.dot(selector, row_data, preferred_element_type=jnp.float32).astype(jnp.bfloat16)


def local_by_slots(tokens, routes, gating, gate_weight, up_weight, down_weight):
    step_count, tok_dev, feature_count = tokens.shape
    topk = routes.shape[2]
    experts_here = gate_weight.shape[0]
    device_count = lax.axis_size("expert")
    experts = experts_here * device_count
    hot_cap = tok_dev * 5 // 8
    outputs = []
    for step_index in range(step_count):
        token_rows = tokens[step_index]
        flat_ids = routes[step_index].reshape(-1)
        ranks = pair_ranks(flat_ids)
        send_slot = flat_ids * hot_cap + ranks
        send_buffer = pack_rows(send_slot, experts * hot_cap, topk, token_rows).reshape(
            device_count, experts_here, hot_cap, token_rows.shape[1]
        )
        results = expert_block(
            lax.all_to_all(send_buffer, "expert", split_axis=0, concat_axis=0, tiled=True),
            gate_weight,
            up_weight,
            down_weight,
        )
        returned = lax.all_to_all(
            results, "expert", split_axis=0, concat_axis=0, tiled=True
        ).reshape(experts * hot_cap, feature_count)
        pair_rows = returned[send_slot]
        weighted = (
            pair_rows.astype(jnp.float32).reshape(tok_dev, topk, feature_count)
            * gating[step_index][:, :, None]
        )
        running = jnp.sum(weighted, axis=1)
        outputs.append(
            lax.psum_scatter(running, "tensor", scatter_dimension=1, tiled=True).astype(
                jnp.bfloat16
            )
        )
    return jnp.stack(outputs)


def solution(mesh):
    body = local if mesh.shape["expert"] == 8 else local_by_slots
    in_specs = (
        P(None, ("groups", "expert"), None),
        P(None, ("groups", "expert"), None),
        P(None, ("groups", "expert"), None),
        P("expert", None, "tensor"),
        P("expert", None, "tensor"),
        P("expert", "tensor", None),
    )
    out_specs = P(None, ("groups", "expert"), "tensor")
    return jax.shard_map(body, mesh=mesh, in_specs=in_specs, out_specs=out_specs, check_vma=False)
```
